256 devices in a mesh: seq: 64 (over z, y, core), head: 4 (over x).
Axes of the slice: x: 4, y: 4, z: 8, core: 2. Of those that a mesh axis runs over, the one named last changes fastest.
Arguments:
- queries: bfloat16 [16, 8192], P(None, 'head'), may hold values from -24 to 24
- keys: bfloat16 [16, 8192, 512], P(None, 'seq', 'head'), may hold values from -24 to 24
- values: bfloat16 [16, 8192, 512], P(None, 'seq', 'head'), may hold values from -8 to 8
- lengths: int32 [16], replicated, may hold values from 2 to 8192, as said below
- residual: bfloat16 [16, 4096], P(None, 'seq'), may hold values from -6 to 6
- out_weight: bfloat16 [8192, 4096], P('head', 'seq'), may hold values from -0.0625 to 0.0625
- norm_gain: float32 [4096], replicated, may hold values from 0.1 to 1.9
- expert_ids: int32 [16, 8], replicated, may hold values from 0 to 63, all different within a row; in each aligned block of 16 rows (0 to 15, 16 to 31, ...) at most 4 rows name the same one
- expert_gates: float32 [16, 8], replicated, may hold values from 0.05 to 0.5
- gate_weight: bfloat16 [64, 4096, 1536], P('seq', None, 'head'), may hold values from -0.09375 to 0.09375
- up_weight: bfloat16 [64, 4096, 1536], P('seq', None, 'head'), may hold values from -0.09375 to 0.09375
- down_weight: bfloat16 [64, 1536, 4096], P('seq', 'head'), may hold values from -0.4375 to 0.4375
Outputs:
- after_attention: bfloat16 [16, 4096], P(None, 'seq')
- layer_out: bfloat16 [16, 4096], P(None, ('seq', 'head'))
The draws below stay inside these ranges and needn't reach their ends.
Inputs may be any that keep to these rules, and one draw needn't show every extreme that they name: `lengths`: at least one row has the full cache length 8192. `expert_ids`: each row names 8 different experts; every expert is named by some row; no expert is named by more than 4 rows, a bound that some block reaches.
All inputs are finite; a program needn't handle non-finite values.
Results may differ from the reference program's by a relative error of at most 0.012.
Values may be sent and summed in bfloat16 or wider, within the bound.
No kernel may reach another device: no remote copies, remote signals or barrier semaphores. Data moves between devices by JAX's collectives and lax.ppermute only.
A program may use at most 64 MiB of HBM per device.

```python
import math
import jax
import jax.numpy as jnp
import numpy as np
from jax import lax

D = 4096
HQ = 64
KVH = 4
HD = 128
FF = 1536
TOPK = 8
ROWS = 16
CTX_DEV = 128
CTX = 8192
EXPERTS = 64
CAP = 4
N_SEQ = 64


def draw_queries(key, part):
    key = jax.random.fold_in(key, 11)
    drawn = jnp.clip(jax.random.normal(key, (ROWS, HQ * HD), jnp.float32), -4.0, 4.0)
    return drawn.astype(jnp.bfloat16)


def draw_keys(key, part):
    key = jax.random.fold_in(key, 12)
    drawn = jnp.clip(jax.random.normal(key, (ROWS, CTX, KVH * HD), jnp.float32), -4.0, 4.0)
    return drawn.astype(jnp.bfloat16)


def draw_values(key, part):
    key = jax.random.fold_in(key, 13)
    first_key, second_key, third_key = jax.random.split(key, 3)
    offsets = jax.random.normal(first_key, (ROWS, 1, KVH * HD), jnp.float32)
    trend_dirs = 1.5 * jnp.clip(jax.random.normal(third_key, (ROWS, 1, KVH * HD), jnp.float32), -3.0, 3.0)
    fraction = (jnp.arange(CTX, dtype=jnp.float32) + 0.5) / CTX
    trend = 2.0 * fraction - 1.0
    drawn = jax.random.normal(second_key, (ROWS, CTX, KVH * HD), jnp.float32) + offsets + trend[None, :, None] * trend_dirs
    return jnp.clip(drawn, -8.0, 8.0).astype(jnp.bfloat16)


def draw_lengths(key, part):
    key = jax.random.fold_in(key, 14)
    first_key, second_key = jax.random.split(key)
    drawn = jax.random.randint(first_key, (ROWS,), 2, CTX + 1, dtype=jnp.int32)
    longest = jax.random.randint(second_key, (), 0, ROWS, dtype=jnp.int32)
    return drawn.at[longest].set(CTX)


def strengthened(result, own_key, source, target, blocks, factor):
    owner, partner = [(jnp.arange(result.shape[dim]) // (result.shape[dim] // blocks)).reshape([-1 if axis == dim else 1 for axis in range(result.ndim)]) for dim in (source, target)]
    chosen = jax.random.permutation(own_key, blocks)[partner]
    strong = (owner == chosen) | (owner == (partner + blocks // 2) % blocks)
    return jnp.where(strong, factor * result, result)


def block_levels(own_key, shape, cuts, smallest, high):
    loudness, own = 1.0, jax.random.fold_in(own_key, 6)
    for axis_at, shards_of in cuts:
        heights = jnp.exp(jax.random.uniform(jax.random.fold_in(own, axis_at), (shards_of,), jnp.float32, smallest / len(cuts), high / len(cuts)))
        loudness = loudness * jnp.repeat(heights, shape[axis_at] // shards_of).reshape([-1 if axis == axis_at else 1 for axis in range(len(shape))])
    return loudness


def routed_block(key, own, number, rows, count, top, bound, lean):
    ranking = jax.random.permutation(key, count)
    heavy_load, common = load_shares(count, rows * top, bound, lean, True), load_shares(count, rows * top, bound, lean, False)
    places = jnp.arange(count)

    def named(sizes, turn):
        used = int((sizes > 0).sum())
        fixed = max(1, used // 4)
        passed = fixed + (places - fixed + turn * (used - fixed)) % max(1, count - fixed)
        return jnp.zeros((count,), jnp.int32).at[ranking[jnp.where(places < fixed, places, passed)]].set(jnp.asarray(sizes, jnp.int32))

    sizes = jnp.where(number % 4 == 0, named(heavy_load, number // 4), named(common, number - number // 4 - 1))
    mixed = jax.random.permutation(jax.random.fold_in(own, 3), count)
    giver, taker = mixed[0:count // 2 * 2:2], mixed[1:count // 2 * 2:2]
    margin = jnp.minimum(sizes[giver] - 1, bound - sizes[taker]) // 2
    margin = jnp.where((giver == ranking[0]) | (taker == ranking[0]) | (sizes[taker] == 0), 0, jnp.maximum(margin, 0))
    passed = jax.random.randint(jax.random.fold_in(own, 4), (count // 2,), 0, 1 << 20) % (margin + 1)
    sizes = sizes.at[giver].add(-passed).at[taker].add(passed)
    labels = jnp.searchsorted(jnp.cumsum(sizes), jnp.arange(rows * top), side="right").astype(jnp.int32)
    listing = labels.reshape(top, rows).T
    listing = listing[jax.random.permutation(jax.random.fold_in(own, 1), rows)]
    turn = jax.random.randint(jax.random.fold_in(own, 2), (rows, 1), 0, top)
    return jnp.take_along_axis(listing, (jnp.arange(top)[None, :] + turn) % top, axis=1)


def load_shares(count, total, limit, skew, full):
    loads = [(1 << 20) // math.isqrt(grade ** skew) + 1 for grade in range(1, count + 1)]
    largest = limit if full else min(limit, max(-(-total // count), total * loads[0] // sum(loads)))
    least = 1 if total - largest >= count - 1 else 0
    counts, spare = [largest] + [least] * (count - 1), total - largest - least * (count - 1)
    while spare > 0:
        candidates = [i for i in range(1, count) if counts[i] < largest] or [i for i in range(1, count) if counts[i] < limit]
        pool, remaining = sum([loads[i] for i in candidates]), spare
        for i in candidates:
            extra = min(limit - counts[i], max(1, remaining * loads[i] // pool), spare)
            counts[i] = counts[i] + extra
            spare = spare - extra
    return np.array(counts)


def gaussian(key, dims, spread, reach, cuts=(), kind=jnp.bfloat16):
    gain = block_levels(key, dims, cuts, -0.22, 0.18) if cuts else 1.0
    values = jax.random.normal(key, dims, jnp.float32) * spread * gain
    return jnp.minimum(jnp.maximum(values, -reach), reach).astype(kind)


def bell_draw_with(key, shape, scale, limit, cuts, heavy, kind=jnp.bfloat16):
    entries = scale * jax.random.normal(key, shape, jnp.float32)
    if cuts:
        entries = entries * block_levels(key, shape, cuts, -0.22, 0.18)
    return jnp.clip(strengthened(entries, jax.random.fold_in(key, 3), *heavy), -limit, limit).astype(kind)


def setup_inputs(seed: int = 0) -> dict:
    key_list = jax.random.split(jax.random.key(seed), 13)
    queries = draw_queries(jax.random.fold_in(key_list[12], 71), 0)
    keys = draw_keys(jax.random.fold_in(key_list[12], 71), 0)
    values = draw_values(jax.random.fold_in(key_list[12], 71), 0)
    lengths = draw_lengths(jax.random.fold_in(key_list[12], 71), 0)
    residual = gaussian(key_list[4], (ROWS, D), 1.0, 6.0, ((1, 64),))
    out_weight = gaussian(key_list[5], (HQ * HD, D), (HQ * HD) ** -0.5, 0.0625, ((0, 4), (1, 64)))
    norm_gain = jnp.clip(1.0 + 0.18 * jax.random.normal(key_list[6], (D,), jnp.float32), 0.1, 1.9)
    expert_ids_keys = jax.random.split(jax.random.fold_in(key_list[7], 1), ROWS // ROWS)
    expert_ids_turns = jax.random.permutation(jax.random.fold_in(key_list[7], 3), ROWS // ROWS)
    expert_ids = jax.vmap(lambda own, number: routed_block(jax.random.fold_in(key_list[7], 2), own, number, ROWS, EXPERTS, TOPK, CAP, 2))(expert_ids_keys, expert_ids_turns).reshape((ROWS, TOPK))
    expert_gates = jnp.clip(jnp.exp(jax.random.uniform(key_list[8], (ROWS, TOPK), jnp.float32, math.log(0.05), math.log(0.5))), 0.05, 0.5)
    gate_weight = gaussian(key_list[9], (EXPERTS, D, FF), D ** -0.5, 0.09375, ((0, 64), (2, 4)))
    up_weight = gaussian(key_list[10], (EXPERTS, D, FF), D ** -0.5, 0.09375, ((0, 64), (2, 4)))
    down_weight = bell_draw_with(key_list[11], (EXPERTS, FF, D), FF ** -0.5, 0.4375, ((0, 64), (1, 4)), (0, 2, 64, 4.0))
    return dict(queries=queries, keys=keys, values=values, lengths=lengths, residual=residual, out_weight=out_weight, norm_gain=norm_gain, expert_ids=expert_ids, expert_gates=expert_gates, gate_weight=gate_weight, up_weight=up_weight, down_weight=down_weight)


masked_value = -1e+30

def reference(queries, keys, values, lengths, residual, out_weight, norm_gain, expert_ids, expert_gates, gate_weight, up_weight, down_weight):
    group_size = HQ // KVH
    query_grid = queries.astype(jnp.float32).reshape(ROWS, KVH, group_size, HD)

    def one_block(block_index):
        start = block_index * CTX_DEV
        key_block = lax.dynamic_slice_in_dim(keys, start, CTX_DEV, 1).astype(jnp.float32).reshape(ROWS, CTX_DEV, KVH, HD)
        value_block = lax.dynamic_slice_in_dim(values, start, CTX_DEV, 1).astype(jnp.float32).reshape(ROWS, CTX_DEV, KVH, HD)
        scores = jnp.einsum('rkgd,rckd->rkgc', query_grid, key_block) * (1.0 / math.sqrt(HD))
        positions = start + jnp.arange(CTX_DEV, dtype=jnp.int32)
        valid_mask = (positions[None, :] < lengths[:, None])[:, None, None, :]
        block_max = lax.optimization_barrier(jnp.max(jnp.where(valid_mask, scores, masked_value), axis=-1))
        weights = jnp.where(valid_mask, jnp.exp(scores - block_max[..., None]), 0.0).astype(jnp.bfloat16)
        weights_wide = weights.astype(jnp.float32)
        block_sum = lax.optimization_barrier(jnp.sum(weights_wide, axis=-1))
        block_numer = jnp.einsum('rkgc,rckd->rkgd', weights_wide, value_block)
        return (block_max, block_sum, block_numer)
    maxima, sums, numers = lax.map(one_block, jnp.arange(N_SEQ, dtype=jnp.int32))
    peak = lax.optimization_barrier(jnp.max(maxima, axis=0))
    scales = jnp.exp(maxima - peak[None])
    weight_total = lax.optimization_barrier(jnp.sum(sums * scales, axis=0))
    numer_total = lax.optimization_barrier(jnp.sum(numers * scales[..., None], axis=0))
    attention = (numer_total / weight_total[..., None]).astype(jnp.bfloat16).reshape(ROWS, HQ * HD)
    projected = jnp.dot(attention, out_weight, preferred_element_type=jnp.float32)
    after_attention = (residual.astype(jnp.float32) + projected).astype(jnp.bfloat16)
    after_wide = after_attention.astype(jnp.float32)
    mean_square = lax.optimization_barrier(jnp.mean(after_wide * after_wide, axis=-1, keepdims=True))
    normed = (after_wide * lax.rsqrt(mean_square + 1e-06) * norm_gain.astype(jnp.float32)).astype(jnp.bfloat16)

    def one_expert(carry, inputs):
        expert_index, gate_matrix, up_matrix, down_matrix = inputs
        gate_proj = jnp.dot(normed, gate_matrix, preferred_element_type=jnp.float32)
        up_proj = jnp.dot(normed, up_matrix, preferred_element_type=jnp.float32)
        hidden = (jax.nn.silu(gate_proj) * up_proj).astype(jnp.bfloat16)
        route_weight = lax.optimization_barrier(jnp.sum(jnp.where(expert_ids == expert_index, expert_gates, 0.0), axis=1)).astype(jnp.float32)
        output = jnp.dot(hidden, down_matrix, preferred_element_type=jnp.float32)
        return (carry + route_weight[:, None] * output, None)
    mixture, unused = lax.scan(one_expert, jnp.zeros((ROWS, D), jnp.float32), (jnp.arange(EXPERTS, dtype=jnp.int32), gate_weight, up_weight, down_weight))
    layer_out = (after_wide + mixture).astype(jnp.bfloat16)
    return (after_attention, layer_out)
```

```python
import math

import jax
import jax.numpy as jnp
from jax import lax
from jax.experimental import pallas as pl
from jax.experimental.pallas import tpu as pltpu
from jax.sharding import PartitionSpec as P

HD = 128
LANES = 128
SLOTS = 4
MASKED = -1e30
CHUNKS = 4
F32 = jnp.float32
BF16 = jnp.bfloat16
NT = (((1,), (1,)), ((), ()))
TN = (((0,), (0,)), ((), ()))


def iota(shape, dim):
    return lax.broadcasted_iota(jnp.int32, shape, dim)


def call(body, outs, args, hbm=(), results=(), scratch=(), limit=8 << 20):
    spaces = [pltpu.HBM if i in hbm else pltpu.VMEM for i in range(len(args))]
    args = [pltpu.with_memory_space_constraint(a, s) for a, s in zip(args, spaces)]
    return pl.pallas_call(
        body,
        out_shape=[
            jax.ShapeDtypeStruct(shape, dtype) if i in results else pltpu.VMEM(shape, dtype)
            for i, (shape, dtype) in enumerate(outs)
        ],
        in_specs=[pl.BlockSpec(memory_space=s) for s in spaces],
        out_specs=[pl.BlockSpec(memory_space=pltpu.VMEM) for _ in outs],
        scratch_shapes=list(scratch),
        compiler_params=pltpu.CompilerParams(vmem_limit_bytes=limit),
    )(*args)


def attend(lengths_hbm, q_hbm, k_hbm, v_hbm, *refs):
    lengths, q, k, v, wide, cache_sems, later_sems = refs[-7:]
    later = (len(refs) - 8) // 2
    out = refs[later]
    rows, heads = q.shape[0], q.shape[1] // HD
    chunk = rows // CHUNKS
    fetch_q = pltpu.make_async_copy(q_hbm, q, cache_sems.at[2 * CHUNKS])
    fetch_q.start()
    fetch_lengths = pltpu.make_async_copy(lengths_hbm, lengths, cache_sems.at[2 * CHUNKS + 1])
    fetch_lengths.start()
    fetch_k, fetch_v = [], []
    for c in range(CHUNKS):
        part = pl.ds(c * chunk, chunk)
        fetch_k.append(pltpu.make_async_copy(k_hbm.at[part], k.at[part], cache_sems.at[c]))
        fetch_k[c].start()
        fetch_v.append(pltpu.make_async_copy(v_hbm.at[part], v.at[part], cache_sems.at[CHUNKS + c]))
        fetch_v[c].start()
    fetch_later = []
    for i in range(later):
        fetch_later.append(pltpu.make_async_copy(refs[i], refs[later + 1 + i], later_sems.at[i]))
        fetch_later[i].start()
    fetch_q.wait()
    for h in range(heads):
        x = q[:, h * HD : (h + 1) * HD].astype(F32)
        at = (h // SLOTS) * 2 * SLOTS + h % SLOTS
        wide[pl.ds(at * rows, rows), :] = x
        wide[pl.ds((at + SLOTS) * rows, rows), :] = x
    fetch_lengths.wait()
    first = lax.axis_index("seq") * k.shape[1]
    tall = 2 * heads
    place = first + iota((tall, k.shape[1]), 1)
    lane = iota((chunk * tall, LANES), 1)
    upper = iota((chunk * tall, LANES), 0) % (2 * SLOTS) < SLOTS
    for c in range(CHUNKS):
        members = range(c * chunk, (c + 1) * chunk)
        fetch_k[c].wait()
        scores = [
            lax.dot_general(
                wide[pl.ds(r, tall, stride=rows), :].astype(BF16), k[r], NT, preferred_element_type=F32
            )
            for r in members
        ]
        scores = jnp.concatenate(scores, axis=0) * (1.0 / math.sqrt(HD))
        valid = jnp.concatenate([place < lengths[r] for r in members], axis=0)
        top = jnp.max(jnp.where(valid, scores, MASKED), axis=1, keepdims=True).astype(BF16).astype(F32)
        weights = jnp.where(valid, jnp.exp(scores - top), 0.0).astype(BF16)
        total = jnp.sum(weights.astype(F32), axis=1, keepdims=True)
        fetch_v[c].wait()
        numer = [
            jnp.dot(weights[i * tall : (i + 1) * tall], v[r], preferred_element_type=F32)
            for i, r in enumerate(members)
        ]
        high = total.astype(BF16).astype(F32)
        stats = jnp.where(lane < 64, top, jnp.where(lane < 96, high, total - high))
        block = jnp.where(upper, jnp.concatenate(numer, axis=0), stats)
        out[pl.ds(c * chunk * tall, chunk * tall), :] = block.astype(BF16)
    for copy in fetch_later:
        copy.wait()


def combine(parts, out):
    count = parts.shape[0] // (2 * SLOTS)
    x = parts[...].astype(F32).reshape(count, 2 * SLOTS, LANES)
    numer, stats = x[:, :SLOTS], x[:, SLOTS:]
    top = stats[:, :, 0:1]
    total = stats[:, :, 64:65] + stats[:, :, 96:97]
    scale = jnp.exp(top - jnp.max(top, axis=0, keepdims=True))
    joined = jnp.sum(scale * numer, axis=0) / jnp.sum(scale * total, axis=0)
    pair = jnp.concatenate([joined, joined], axis=0)
    out[...] = jnp.broadcast_to(pair[None], (count // 2, 2 * SLOTS, LANES)).reshape(out.shape).astype(BF16)


def project(pieces, weight, out, wide):
    rows = 2 * out.shape[1]
    heads = pieces.shape[0] // rows
    wide[...] = pieces[...].astype(F32)
    lhs = jnp.concatenate(
        [wide[pl.ds(h, rows, stride=heads), :].astype(BF16) for h in range(heads)], axis=1
    )
    part = lax.dot_general(lhs, weight[...], NT, preferred_element_type=F32)
    halves = jnp.concatenate([part[: rows // 2], part[rows // 2 :]], axis=1)
    out[...] = jnp.broadcast_to(halves[None], out.shape)


def selection(ids, count, copies):
    top_k, rows = ids.shape
    shape = (count * copies * 2, 2 * rows)
    expert = iota(shape, 0) // (2 * copies)
    wide = jnp.concatenate([ids, ids], axis=1)
    hit = expert == wide[0:1, :]
    for k in range(1, top_k):
        hit = hit | (expert == wide[k : k + 1, :])
    hit = hit.astype(F32)
    square = (2 * rows, 2 * rows)
    before = (iota(square, 0) < iota(square, 1) % rows).astype(F32)
    rank = jnp.dot(hit, before, preferred_element_type=F32)
    slot = iota(shape, 0) % 2 + 2 * (iota(shape, 1) // rows)
    return jnp.where(rank == slot.astype(F32), hit, 0.0).astype(BF16)


def residual_step(parts, residual, ids, after, out):
    total = parts[0]
    for i in range(1, parts.shape[0]):
        total = total + parts[i]
    total = jnp.concatenate([total[:, : LANES // 2], total[:, LANES // 2 :]], axis=0)
    own = (residual[...].astype(F32) + total).astype(BF16)
    after[...] = own
    own = own.astype(F32)
    none = jnp.zeros_like(own)
    twice = jnp.concatenate(
        [jnp.concatenate([own, none], axis=1), jnp.concatenate([none, own], axis=1)], axis=0
    ).astype(BF16)
    pick = selection(ids[...], out.shape[0] // 2, 1)
    out[...] = jnp.dot(pick, twice, preferred_element_type=F32).astype(BF16)


def swap(y):
    count = y.shape[0]
    row = iota(y.shape, 0) % 4
    lane = iota(y.shape, 1)
    z = pltpu.roll(y, 64, 1)
    up = pltpu.roll(z, count - 2, 0)
    down = pltpu.roll(z, 2, 0)
    return jnp.where(lane < 64, jnp.where(row < 2, y, down), jnp.where(row < 2, up, y))


def experts(pieces, gain, gate, up, down, ids, gates, out):
    width = gain.shape[1]
    blocks = width // LANES
    stacked = swap(pieces[...].astype(F32))
    tiles = []
    for b in range(blocks):
        tile = stacked[8 * (b // 2) : 8 * (b // 2) + 8]
        tiles.append(tile if b % 2 == 0 else pltpu.roll(tile, 4, 0))
    x = jnp.concatenate(tiles, axis=1)
    square = jnp.sum(x * x, axis=1, keepdims=True) * (1.0 / width)
    normed = (x * lax.rsqrt(square + 1e-6) * gain[...]).astype(BF16)
    gate_proj = jnp.dot(normed, gate[0], preferred_element_type=F32)
    up_proj = jnp.dot(normed, up[0], preferred_element_type=F32)
    hidden = (gate_proj / (1.0 + jnp.exp(-gate_proj)) * up_proj).astype(BF16)
    result = jnp.dot(hidden, down[0], preferred_element_type=F32)

    rows = ids.shape[1]
    mine = ids[...] == lax.axis_index("seq")
    route = jnp.sum(jnp.where(mine, gates[...], 0.0), axis=0, keepdims=True)
    named = jnp.max(mine.astype(F32), axis=0, keepdims=True)
    named = jnp.broadcast_to(named, (8, rows))
    before = (iota((rows, rows), 0) < iota((rows, rows), 1)).astype(F32)
    rank = jnp.dot(named, before, preferred_element_type=F32)
    chosen = (rank == iota((8, rows), 0).astype(F32)) & (named > 0.0)
    result = result * jnp.sum(jnp.where(chosen, route, 0.0), axis=1, keepdims=True)

    lower = iota((8, LANES), 0) < 4
    pairs = []
    for b in range(0, blocks, 2):
        left = result[:, b * LANES : (b + 1) * LANES]
        right = result[:, (b + 1) * LANES : (b + 2) * LANES]
        pairs.append(jnp.where(lower, left, pltpu.roll(right, 4, 0)))
    packed = swap(jnp.concatenate(pairs, axis=0)).astype(BF16)
    shape = (out.shape[0], packed.shape[0])
    copies = out.shape[0] // packed.shape[0]
    target, source = iota(shape, 0), iota(shape, 1)
    repeat = (target // (2 * copies) == source // 2) & (target % 2 == source % 2)
    out[...] = jnp.dot(repeat.astype(BF16), packed, preferred_element_type=F32).astype(BF16)


def finish(pieces, after, ids, out):
    rows, width = out.shape
    pick = selection(ids[...], 64, pieces.shape[0] // 128)
    mixed = lax.dot_general(pick, pieces[...], TN, preferred_element_type=F32)
    mixture = mixed[:rows] + pltpu.roll(mixed[rows:], 64, 1)
    own = after[...].astype(F32)
    total = mixture + jnp.concatenate([own, jnp.zeros_like(own)], axis=1)
    shift = (LANES - width * lax.axis_index("head")) % LANES
    out[...] = pltpu.roll(total, shift, 1)[:, :width].astype(BF16)


def exchange(x, axis):
    return lax.all_to_all(x, axis, 0, 0, tiled=True)


def local(
    queries,
    keys,
    values,
    lengths,
    residual,
    out_weight,
    norm_gain,
    expert_ids,
    expert_gates,
    gate_weight,
    up_weight,
    down_weight,
):
    seq, head = lax.axis_size("seq"), lax.axis_size("head")
    rows = queries.shape[0]
    ids, gates = expert_ids.T, expert_gates.T

    later = [out_weight.T, residual, norm_gain.reshape(1, -1), ids, gates, gate_weight, up_weight, down_weight]
    parts, *later = call(
        attend,
        [((seq * 2 * SLOTS, LANES), BF16)] + [(a.shape, a.dtype) for a in later],
        [lengths, queries, keys, values, *later],
        hbm=range(4 + len(later)),
        scratch=[
            pltpu.SMEM(lengths.shape, lengths.dtype),
            pltpu.VMEM(queries.shape, BF16),
            pltpu.VMEM(keys.shape, BF16),
            pltpu.VMEM(values.shape, BF16),
            pltpu.VMEM((2 * queries.shape[1] // HD * rows, HD), F32),
            pltpu.SemaphoreType.DMA((2 * CHUNKS + 2,)),
            pltpu.SemaphoreType.DMA((len(later),)),
        ],
    )
    weight, residual, gain, ids, gates, gate_weight, up_weight, down_weight = later
    parts = exchange(parts, "seq")
    (joined,) = call(combine, [((seq * SLOTS, LANES), BF16)], [parts])
    joined = exchange(joined, "seq")
    (projected,) = call(
        project,
        [((head, rows // 2, LANES), F32)],
        [joined, weight],
        scratch=[pltpu.VMEM((seq * SLOTS, LANES), F32)],
    )
    summands = exchange(projected, "head")
    after, chosen = call(
        residual_step,
        [(residual.shape, BF16), ((seq * 2, LANES), BF16)],
        [summands, residual, ids],
    )
    chosen = exchange(chosen, "seq")
    (outputs,) = call(
        experts,
        [((seq * head * 2, LANES), BF16)],
        [chosen, gain, gate_weight, up_weight, down_weight, ids, gates],
    )
    outputs = exchange(outputs, ("seq", "head"))
    (layer_out,) = call(
        finish, [((rows, residual.shape[1] // head), BF16)], [outputs, after, ids], results=(0,)
    )
    return after, layer_out


def solution(mesh):
    in_specs = (
        P(None, "head"),
        P(None, "seq", "head"),
        P(None, "seq", "head"),
        P(),
        P(None, "seq"),
        P("head", "seq"),
        P(),
        P(),
        P(),
        P("seq", None, "head"),
        P("seq", None, "head"),
        P("seq", "head", None),
    )
    out_specs = (P(None, "seq"), P(None, ("seq", "head")))
    return jax.shard_map(local, mesh=mesh, in_specs=in_specs, out_specs=out_specs, check_vma=False)
```

```python
import math

import jax
import jax.numpy as jnp
from jax import lax
from jax.experimental import pallas as pl
from jax.experimental.pallas import tpu as pltpu
from jax.sharding import PartitionSpec as P

HD = 128
LANES = 128
SLOTS = 4
MASKED = -1e30
CHUNKS = 1
STREAMS = 4
F32 = jnp.float32
BF16 = jnp.bfloat16
NT = (((1,), (1,)), ((), ()))
TN = (((0,), (0,)), ((), ()))


def iota(shape, dim):
    return lax.broadcasted_iota(jnp.int32, shape, dim)


def call(body, outs, args, hbm=(), results=(), scratch=(), limit=16 << 20):
    spaces = [pltpu.HBM if i in hbm else pltpu.VMEM for i in range(len(args))]
    args = [pltpu.with_memory_space_constraint(a, s) for a, s in zip(args, spaces)]
    return pl.pallas_call(
        body,
        out_shape=[
            jax.ShapeDtypeStruct(shape, dtype) if i in results else pltpu.VMEM(shape, dtype)
            for i, (shape, dtype) in enumerate(outs)
        ],
        in_specs=[pl.BlockSpec(memory_space=s) for s in spaces],
        out_specs=[pl.BlockSpec(memory_space=pltpu.VMEM) for _ in outs],
        scratch_shapes=list(scratch),
        compiler_params=pltpu.CompilerParams(vmem_limit_bytes=limit),
    )(*args)


def attend(lengths_hbm, q_hbm, k_hbm, v_hbm, *refs):
    lengths, q, k, v, wide, cache_sems, later_sems = refs[-7:]
    later = (len(refs) - 8) // 2
    out = refs[later]
    rows, heads = q.shape[0], q.shape[1] // HD
    chunk = rows // CHUNKS
    fetch_q = pltpu.make_async_copy(q_hbm, q, cache_sems.at[2 * CHUNKS])
    fetch_q.start()
    fetch_lengths = pltpu.make_async_copy(lengths_hbm, lengths, cache_sems.at[2 * CHUNKS + 1])
    fetch_lengths.start()
    fetch_k, fetch_v = [], []
    for c in range(CHUNKS):
        part = pl.ds(c * chunk, chunk)
        fetch_k.append(pltpu.make_async_copy(k_hbm.at[part], k.at[part], cache_sems.at[c]))
        fetch_k[c].start()
        fetch_v.append(pltpu.make_async_copy(v_hbm.at[part], v.at[part], cache_sems.at[CHUNKS + c]))
        fetch_v[c].start()
    fetch_later = []
    for i in range(later):
        fetch_later.append(pltpu.make_async_copy(refs[i], refs[later + 1 + i], later_sems.at[i]))
        fetch_later[i].start()
    fetch_q.wait()
    for h in range(heads):
        x = q[:, h * HD : (h + 1) * HD].astype(F32)
        at = (h // SLOTS) * 2 * SLOTS + h % SLOTS
        wide[pl.ds(at * rows, rows), :] = x
        wide[pl.ds((at + SLOTS) * rows, rows), :] = x
    fetch_lengths.wait()
    first = lax.axis_index("seq") * k.shape[1]
    tall = 2 * heads
    place = first + iota((tall, k.shape[1]), 1)
    lane = iota((chunk * tall, LANES), 1)
    upper = iota((chunk * tall, LANES), 0) % (2 * SLOTS) < SLOTS
    for c in range(CHUNKS):
        members = range(c * chunk, (c + 1) * chunk)
        fetch_k[c].wait()
        scores = [
            lax.dot_general(
                wide[pl.ds(r, tall, stride=rows), :].astype(BF16), k[r], NT, preferred_element_type=F32
            )
            for r in members
        ]
        scores = jnp.concatenate(scores, axis=0) * (1.0 / math.sqrt(HD))
        valid = jnp.concatenate([place < lengths[r] for r in members], axis=0)
        top = jnp.max(jnp.where(valid, scores, MASKED), axis=1, keepdims=True).astype(BF16).astype(F32)
        weights = jnp.where(valid, jnp.exp(scores - top), 0.0).astype(BF16)
        total = jnp.sum(weights.astype(F32), axis=1, keepdims=True)
        fetch_v[c].wait()
        numer = [
            jnp.dot(weights[i * tall : (i + 1) * tall], v[r], preferred_element_type=F32)
            for i, r in enumerate(members)
        ]
        high = total.astype(BF16).astype(F32)
        stats = jnp.where(lane < 64, top, jnp.where(lane < 96, high, total - high))
        block = jnp.where(upper, jnp.concatenate(numer, axis=0), stats)
        out[pl.ds(c * chunk * tall, chunk * tall), :] = block.astype(BF16)
    for copy in fetch_later:
        copy.wait()


def combine(parts, out):
    count = parts.shape[0] // (2 * SLOTS)
    x = parts[...].astype(F32).reshape(count, 2 * SLOTS, LANES)
    numer, stats = x[:, :SLOTS], x[:, SLOTS:]
    top = stats[:, :, 0:1]
    total = stats[:, :, 64:65] + stats[:, :, 96:97]
    scale = jnp.exp(top - jnp.max(top, axis=0, keepdims=True))
    joined = jnp.sum(scale * numer, axis=0) / jnp.sum(scale * total, axis=0)
    pair = jnp.concatenate([joined, joined], axis=0)
    out[...] = jnp.broadcast_to(pair[None], (count // 2, 2 * SLOTS, LANES)).reshape(out.shape).astype(BF16)


def project(pieces, weight, residual, ids, out, pick, wide):
    rows = residual.shape[0]
    heads = pieces.shape[0] // rows
    wide[...] = pieces[...].astype(F32)
    lhs = jnp.concatenate(
        [wide[pl.ds(h, rows, stride=heads), :].astype(BF16) for h in range(heads)], axis=1
    )
    part = lax.dot_general(lhs, weight[...], NT, preferred_element_type=F32)
    part = part + jnp.where(lax.axis_index("head") == 0, residual[...].astype(F32), 0.0)
    none = jnp.zeros_like(part)
    twice = jnp.concatenate(
        [jnp.concatenate([part, none], axis=1), jnp.concatenate([none, part], axis=1)], axis=0
    ).astype(BF16)
    chosen = selection(ids[...], pick.shape[0] // 2)
    pick[...] = chosen
    send = jnp.dot(chosen, twice, preferred_element_type=F32).astype(BF16)
    out[...] = jnp.concatenate([send] * (out.shape[0] // send.shape[0]), axis=0)


def selection(ids, count):
    top_k, rows = ids.shape
    shape = (count * 2, 2 * rows)
    expert = iota(shape, 0) // 2
    wide = jnp.concatenate([ids, ids], axis=1)
    hit = expert == wide[0:1, :]
    for k in range(1, top_k):
        hit = hit | (expert == wide[k : k + 1, :])
    hit = hit.astype(F32)
    square = (2 * rows, 2 * rows)
    before = (iota(square, 0) < iota(square, 1) % rows).astype(F32)
    rank = jnp.dot(hit, before, preferred_element_type=F32)
    slot = iota(shape, 0) % 2 + 2 * (iota(shape, 1) // rows)
    return jnp.where(rank == slot.astype(F32), hit, 0.0).astype(BF16)


def swap(y):
    count = y.shape[0]
    row = iota(y.shape, 0) % 4
    lane = iota(y.shape, 1)
    z = pltpu.roll(y, 64, 1)
    up = pltpu.roll(z, count - 2, 0)
    down = pltpu.roll(z, 2, 0)
    return jnp.where(lane < 64, jnp.where(row < 2, y, down), jnp.where(row < 2, up, y))


def experts(pieces, gain, down, ids, gates, gate_hbm, up_hbm, out, gate, up, sems):
    width = gain.shape[1]
    blocks = width // LANES
    depth = gate.shape[0] // STREAMS
    fetch = []
    for i in range(STREAMS):
        part = pl.ds(i * depth, depth)
        fetch.append(pltpu.make_async_copy(gate_hbm.at[0, part], gate.at[part], sems.at[2 * i]))
        fetch.append(pltpu.make_async_copy(up_hbm.at[0, part], up.at[part], sems.at[2 * i + 1]))
    for copy in fetch:
        copy.start()
    half = 2 * lax.axis_size("seq")
    heads = pieces.shape[0] // half
    summed = pieces[:half].astype(F32)
    for i in range(1, heads):
        summed = summed + pieces[i * half : (i + 1) * half].astype(F32)
    stacked = swap(summed).astype(BF16).astype(F32)
    tiles = []
    for b in range(blocks):
        tile = stacked[8 * (b // 2) : 8 * (b // 2) + 8]
        tiles.append(tile if b % 2 == 0 else pltpu.roll(tile, 4, 0))
    x = jnp.concatenate(tiles, axis=1)
    square = jnp.sum(x * x, axis=1, keepdims=True) * (1.0 / width)
    normed = (x * lax.rsqrt(square + 1e-6) * gain[...]).astype(BF16)
    gate_proj = up_proj = jnp.zeros((normed.shape[0], gate.shape[1]), F32)
    for i in range(STREAMS):
        part = slice(i * depth, (i + 1) * depth)
        fetch[2 * i].wait()
        gate_proj = gate_proj + jnp.dot(normed[:, part], gate[part], preferred_element_type=F32)
        fetch[2 * i + 1].wait()
        up_proj = up_proj + jnp.dot(normed[:, part], up[part], preferred_element_type=F32)
    hidden = (gate_proj / (1.0 + jnp.exp(-gate_proj)) * up_proj).astype(BF16)
    result = jnp.dot(hidden, down[0], preferred_element_type=F32)

    rows = ids.shape[1]
    mine = ids[...] == lax.axis_index("seq")
    route = jnp.sum(jnp.where(mine, gates[...], 0.0), axis=0, keepdims=True)
    named = jnp.max(mine.astype(F32), axis=0, keepdims=True)
    named = jnp.broadcast_to(named, (8, rows))
    before = (iota((rows, rows), 0) < iota((rows, rows), 1)).astype(F32)
    rank = jnp.dot(named, before, preferred_element_type=F32)
    chosen = (rank == iota((8, rows), 0).astype(F32)) & (named > 0.0)
    result = result * jnp.sum(jnp.where(chosen, route, 0.0), axis=1, keepdims=True)

    lower = iota((8, LANES), 0) < 4
    pairs = []
    for b in range(0, blocks, 2):
        left = result[:, b * LANES : (b + 1) * LANES]
        right = result[:, (b + 1) * LANES : (b + 2) * LANES]
        pairs.append(jnp.where(lower, left, pltpu.roll(right, 4, 0)))
    mixed = jnp.concatenate(pairs, axis=0)
    head = lax.axis_index("head")
    group = iota(mixed.shape, 1) // 16 % heads
    moved = pltpu.roll(stacked, jnp.where(head % 2 == 0, 16, LANES - 16), 1)
    for target in range(heads):
        carried = jnp.where(target == head, moved, stacked)
        packed = swap(jnp.where(group == target, mixed, carried))
        out[pl.ds(target * half, half), :] = packed.astype(BF16)


def finish(pieces, pick, ids, after, out):
    half = pick.shape[0]
    rows, width = out.shape
    heads = pieces.shape[0] // half
    chosen = pick[...]
    first = jnp.concatenate([ids[0:1, :], ids[0:1, :]], axis=1) == iota(chosen.shape, 0) // 2
    both = jnp.concatenate([chosen.astype(F32), jnp.where(first, chosen.astype(F32), 0.0)], axis=1).astype(BF16)
    head = lax.axis_index("head")
    group = iota((rows, LANES), 1) // 16
    mixture = jnp.zeros((rows, LANES), F32)
    own = jnp.zeros((rows, LANES), F32)
    for source in range(heads):
        got = lax.dot_general(both, pieces[source * half : (source + 1) * half], TN, preferred_element_type=F32)
        mixture = mixture + got[:rows] + pltpu.roll(got[rows : 2 * rows], 64, 1)
        carried = got[2 * rows : 3 * rows] + pltpu.roll(got[3 * rows :], 64, 1)
        moved = pltpu.roll(carried, LANES - 16 if source % 2 == 0 else 16, 1)
        own = own + jnp.where(group == source, jnp.where(head == source, moved, carried), 0.0)
    after[...] = own[:, : after.shape[1]].astype(BF16)
    shift = (LANES - width * head) % LANES
    out[...] = pltpu.roll(mixture + own, shift, 1)[:, :width].astype(BF16)


def exchange(x, axis):
    return lax.all_to_all(x, axis, 0, 0, tiled=True)


def local(
    queries,
    keys,
    values,
    lengths,
    residual,
    out_weight,
    norm_gain,
    expert_ids,
    expert_gates,
    gate_weight,
    up_weight,
    down_weight,
):
    seq, head = lax.axis_size("seq"), lax.axis_size("head")
    rows = queries.shape[0]
    ids, gates = expert_ids.T, expert_gates.T

    later = [out_weight.T, residual, norm_gain.reshape(1, -1), ids, gates, down_weight]
    parts, *later = call(
        attend,
        [((seq * 2 * SLOTS, LANES), BF16)] + [(a.shape, a.dtype) for a in later],
        [lengths, queries, keys, values, *later],
        hbm=range(4 + len(later)),
        scratch=[
            pltpu.SMEM(lengths.shape, lengths.dtype),
            pltpu.VMEM(queries.shape, BF16),
            pltpu.VMEM(keys.shape, BF16),
            pltpu.VMEM(values.shape, BF16),
            pltpu.VMEM((2 * queries.shape[1] // HD * rows, HD), F32),
            pltpu.SemaphoreType.DMA((2 * CHUNKS + 2,)),
            pltpu.SemaphoreType.DMA((len(later),)),
        ],
    )
    weight, residual, gain, ids, gates, down_weight = later
    parts = exchange(parts, "seq")
    (joined,) = call(combine, [((seq * SLOTS, LANES), BF16)], [parts])
    joined = exchange(joined, "seq")
    chosen, pick = call(
        project,
        [((head * seq * 2, LANES), BF16), ((seq * 2, 2 * rows), BF16)],
        [joined, weight, residual, ids],
        scratch=[pltpu.VMEM((seq * SLOTS, LANES), F32)],
    )
    chosen = exchange(chosen, ("head", "seq"))
    (outputs,) = call(
        experts,
        [((head * seq * 2, LANES), BF16)],
        [chosen, gain, down_weight, ids, gates, gate_weight, up_weight],
        hbm=(5, 6),
        scratch=[
            pltpu.VMEM(gate_weight.shape[1:], BF16),
            pltpu.VMEM(up_weight.shape[1:], BF16),
            pltpu.SemaphoreType.DMA((2 * STREAMS,)),
        ],
    )
    outputs = exchange(outputs, ("head", "seq"))
    return call(
        finish,
        [(residual.shape, BF16), ((rows, residual.shape[1] // head), BF16)],
        [outputs, pick, ids],
        results=(0, 1),
    )


def solution(mesh):
    in_specs = (
        P(None, "head"),
        P(None, "seq", "head"),
        P(None, "seq", "head"),
        P(),
        P(None, "seq"),
        P("head", "seq"),
        P(),
        P(),
        P(),
        P("seq", None, "head"),
        P("seq", None, "head"),
        P("seq", "head", None),
    )
    out_specs = (P(None, "seq"), P(None, ("seq", "head")))
    return jax.shard_map(local, mesh=mesh, in_specs=in_specs, out_specs=out_specs, check_vma=False)
```

```python
import math

import jax
import jax.numpy as jnp
from jax import lax
from jax.experimental import pallas as pl
from jax.experimental.pallas import tpu as pltpu
from jax.sharding import PartitionSpec as P

HD = 128
LANES = 128
SLOTS = 4
MASKED = -1e30
F32 = jnp.float32
BF16 = jnp.bfloat16
NT = (((1,), (1,)), ((), ()))


def iota(shape, dim):
    return lax.broadcasted_iota(jnp.int32, shape, dim)


def call(body, outs, args, hbm=(), results=(), scratch=(), limit=16 << 20, cost=None):
    spaces = [pltpu.HBM if i in hbm else pltpu.VMEM for i in range(len(args))]
    args = [pltpu.with_memory_space_constraint(a, s) if s is pltpu.HBM else a for a, s in zip(args, spaces)]
    return pl.pallas_call(
        body,
        out_shape=[
            jax.ShapeDtypeStruct(shape, dtype) if i in results else pltpu.VMEM(shape, dtype)
            for i, (shape, dtype) in enumerate(outs)
        ],
        in_specs=[pl.BlockSpec(memory_space=s) for s in spaces],
        out_specs=[pl.BlockSpec(memory_space=pltpu.VMEM) for _ in outs],
        scratch_shapes=list(scratch),
        compiler_params=pltpu.CompilerParams(vmem_limit_bytes=limit),
        cost_estimate=cost,
    )(*args)


def attend(lengths_hbm, q_hbm, k_hbm, v_hbm, ids_hbm, gates_hbm, *refs):
    lengths, q, k, v, ids, gates, wide, sems = refs[-8:]
    later = (len(refs) - 12) // 2
    out, pick, turned, route = refs[2 * later : -8]
    rows, heads = q.shape[0], q.shape[1] // HD
    pairs = [(ids_hbm, ids), (gates_hbm, gates), (q_hbm, q), (k_hbm, k), (lengths_hbm, lengths), (v_hbm, v)]
    pairs += [(refs[i], refs[later + i]) for i in range(later)]
    fetch = [pltpu.make_async_copy(far, near, sems.at[i]) for i, (far, near) in enumerate(pairs)]
    for copy in fetch:
        copy.start()
    fetch[0].wait()
    fetch[1].wait()
    routing(ids[...], gates[...], pick, turned, route)
    fetch[2].wait()
    for h in range(heads):
        x = q[:, h * HD : (h + 1) * HD].astype(F32)
        at = (h // SLOTS) * 2 * SLOTS + h % SLOTS
        wide[pl.ds(at * rows, rows), :] = x
        wide[pl.ds((at + SLOTS) * rows, rows), :] = x
    tall = 2 * heads
    lane = iota((rows * tall, LANES), 1)
    upper = iota((rows * tall, LANES), 0) % (2 * SLOTS) < SLOTS
    fetch[3].wait()
    scores = [
        lax.dot_general(
            wide[pl.ds(r, tall, stride=rows), :].astype(BF16), k[r], NT, preferred_element_type=F32
        )
        for r in range(rows)
    ]
    scores = jnp.concatenate(scores, axis=0) * (1.0 / math.sqrt(HD))
    fetch[4].wait()
    place = lax.axis_index("seq") * k.shape[1] + iota((tall, k.shape[1]), 1)
    valid = jnp.concatenate([place < lengths[r] for r in range(rows)], axis=0)
    top = jnp.max(jnp.where(valid, scores, MASKED), axis=1, keepdims=True).astype(BF16).astype(F32)
    weights = jnp.where(valid, jnp.exp(scores - top), 0.0).astype(BF16)
    total = jnp.sum(weights.astype(F32), axis=1, keepdims=True)
    fetch[5].wait()
    numer = [
        jnp.dot(weights[r * tall : (r + 1) * tall], v[r], preferred_element_type=F32)
        for r in range(rows)
    ]
    high = total.astype(BF16).astype(F32)
    stats = jnp.where(lane < 64, top, jnp.where(lane < 96, high, total - high))
    out[...] = jnp.where(upper, jnp.concatenate(numer, axis=0), stats).astype(BF16)
    for copy in fetch[6:]:
        copy.wait()


def routing(ids, gates, pick, turned, route):
    chosen = selection(ids, pick.shape[0] // 2)
    pick[...] = chosen.astype(BF16)
    first = jnp.concatenate([ids[0:1, :], ids[0:1, :]], axis=1) == iota(chosen.shape, 0) // 2
    first = jnp.where(first, chosen, 0.0)
    both = jnp.concatenate([chosen, first, jnp.zeros((pick.shape[0], LANES - 2 * pick.shape[1]), F32)], axis=1)
    turned[...] = both.T[: turned.shape[0]].astype(BF16)

    rows = ids.shape[1]
    mine = ids == lax.axis_index("seq")
    gate = jnp.sum(jnp.where(mine, gates, 0.0), axis=0, keepdims=True)
    here = jnp.broadcast_to(jnp.max(mine.astype(F32), axis=0, keepdims=True), (8, rows))
    before = (iota((rows, rows), 0) < iota((rows, rows), 1)).astype(F32)
    rank = jnp.dot(here, before, preferred_element_type=F32)
    taken = (rank == iota((8, rows), 0).astype(F32)) & (here > 0.0)
    weight = jnp.sum(jnp.where(taken, gate, 0.0), axis=1, keepdims=True)
    route[...] = jnp.broadcast_to(weight, route.shape)


def combine(parts, out):
    count = parts.shape[0] // (2 * SLOTS)
    x = parts[...].astype(F32).reshape(count, 2 * SLOTS, LANES)
    numer, stats = x[:, :SLOTS], x[:, SLOTS:]
    top = stats[:, :, 0:1]
    total = stats[:, :, 64:65] + stats[:, :, 96:97]
    scale = jnp.exp(top - jnp.max(top, axis=0, keepdims=True))
    joined = jnp.sum(scale * numer, axis=0) / jnp.sum(scale * total, axis=0)
    pair = jnp.concatenate([joined, joined], axis=0)
    out[...] = jnp.broadcast_to(pair[None], (count // 2, 2 * SLOTS, LANES)).reshape(out.shape).astype(BF16)


def project(pieces, weight, residual, pick, out, wide):
    rows = residual.shape[0]
    heads = pieces.shape[0] // rows
    wide[...] = pieces[...].astype(F32)
    lhs = jnp.concatenate(
        [wide[pl.ds(h, rows, stride=heads), :].astype(BF16) for h in range(heads)], axis=1
    )
    part = lax.dot_general(lhs, weight[...], NT, preferred_element_type=F32)
    part = part + jnp.where(lax.axis_index("head") == 0, residual[...].astype(F32), 0.0)
    none = jnp.zeros_like(part)
    twice = jnp.concatenate(
        [jnp.concatenate([part, none], axis=1), jnp.concatenate([none, part], axis=1)], axis=0
    ).astype(BF16)
    send = jnp.dot(pick[...], twice, preferred_element_type=F32).astype(BF16)
    out[...] = jnp.concatenate([send] * (out.shape[0] // send.shape[0]), axis=0)


def selection(ids, count):
    top_k, rows = ids.shape
    shape = (count * 2, 2 * rows)
    expert = iota(shape, 0) // 2
    wide = jnp.concatenate([ids, ids], axis=1)
    hit = expert == wide[0:1, :]
    for k in range(1, top_k):
        hit = hit | (expert == wide[k : k + 1, :])
    hit = hit.astype(F32)
    square = (2 * rows, 2 * rows)
    before = (iota(square, 0) < iota(square, 1) % rows).astype(F32)
    rank = jnp.dot(hit, before, preferred_element_type=F32)
    slot = iota(shape, 0) % 2 + 2 * (iota(shape, 1) // rows)
    return jnp.where(rank == slot.astype(F32), hit, 0.0)


def swap(y):
    count = y.shape[0]
    row = iota(y.shape, 0) % 4
    lane = iota(y.shape, 1)
    z = pltpu.roll(y, 64, 1)
    up = pltpu.roll(z, count - 2, 0)
    down = pltpu.roll(z, 2, 0)
    return jnp.where(lane < 64, jnp.where(row < 2, y, down), jnp.where(row < 2, up, y))


def experts(pieces, gain, gate, up, down, route, out):
    width = gain.shape[1]
    blocks = width // LANES
    half = 2 * lax.axis_size("seq")
    heads = pieces.shape[0] // half
    summed = pieces[:half].astype(F32)
    for i in range(1, heads):
        summed = summed + pieces[i * half : (i + 1) * half].astype(F32)
    stacked = swap(summed).astype(BF16).astype(F32)
    tiles = []
    for b in range(blocks):
        tile = stacked[8 * (b // 2) : 8 * (b // 2) + 8]
        tiles.append(tile if b % 2 == 0 else pltpu.roll(tile, 4, 0))
    x = jnp.concatenate(tiles, axis=1)
    square = jnp.sum(x * x, axis=1, keepdims=True) * (1.0 / width)
    normed = (x * lax.rsqrt(square + 1e-6) * gain[...]).astype(BF16)
    gate_proj = jnp.dot(normed, gate[0], preferred_element_type=F32)
    up_proj = jnp.dot(normed, up[0], preferred_element_type=F32)
    hidden = (gate_proj / (1.0 + jnp.exp(-gate_proj)) * up_proj).astype(BF16)
    result = jnp.dot(hidden, down[0], preferred_element_type=F32) * route[:, 0:1]

    lower = iota((8, LANES), 0) < 4
    pairs = []
    for b in range(0, blocks, 2):
        left = result[:, b * LANES : (b + 1) * LANES]
        right = result[:, (b + 1) * LANES : (b + 2) * LANES]
        pairs.append(jnp.where(lower, left, pltpu.roll(right, 4, 0)))
    mixed = jnp.concatenate(pairs, axis=0)
    head = lax.axis_index("head")
    group = iota(mixed.shape, 1) // 16 % heads
    moved = pltpu.roll(stacked, jnp.where(head % 2 == 0, 16, LANES - 16), 1)
    for target in range(heads):
        carried = jnp.where(target == head, moved, stacked)
        packed = swap(jnp.where(group == target, mixed, carried))
        out[pl.ds(target * half, half), :] = packed.astype(BF16)


def finish(pieces, turned, after, out):
    half = turned.shape[1]
    rows, width = out.shape
    heads = pieces.shape[0] // half
    head = lax.axis_index("head")
    group = iota((rows, LANES), 1) // 16
    mixture = jnp.zeros((rows, LANES), F32)
    own = jnp.zeros((rows, LANES), F32)
    for source in range(heads):
        got = jnp.dot(turned[...], pieces[source * half : (source + 1) * half], preferred_element_type=F32)
        mixture = mixture + got[:rows] + pltpu.roll(got[rows : 2 * rows], 64, 1)
        carried = got[2 * rows : 3 * rows] + pltpu.roll(got[3 * rows :], 64, 1)
        moved = pltpu.roll(carried, LANES - 16 if source % 2 == 0 else 16, 1)
        own = own + jnp.where(group == source, jnp.where(head == source, moved, carried), 0.0)
    after[...] = own[:, : after.shape[1]].astype(BF16)
    shift = (LANES - width * head) % LANES
    out[...] = pltpu.roll(mixture + own, shift, 1)[:, :width].astype(BF16)


def exchange(x, axis):
    return lax.all_to_all(x, axis, 0, 0, tiled=True)


def local(
    queries,
    keys,
    values,
    lengths,
    residual,
    out_weight,
    norm_gain,
    expert_ids,
    expert_gates,
    gate_weight,
    up_weight,
    down_weight,
):
    seq, head = lax.axis_size("seq"), lax.axis_size("head")
    rows = queries.shape[0]
    later = [out_weight.T, residual, norm_gain.reshape(1, -1)]
    weight, residual, gain, parts, pick, turned, route = call(
        attend,
        [(a.shape, a.dtype) for a in later]
        + [((seq * 2 * SLOTS, LANES), BF16)]
        + [((seq * 2, 2 * rows), BF16), ((4 * rows, seq * 2), BF16), ((8, LANES), F32)],
        [lengths, queries, keys, values, expert_ids.T, expert_gates.T, *later],
        hbm=range(6 + len(later)),
        scratch=[
            pltpu.SMEM(lengths.shape, lengths.dtype),
            pltpu.VMEM(queries.shape, BF16),
            pltpu.VMEM(keys.shape, BF16),
            pltpu.VMEM(values.shape, BF16),
            pltpu.VMEM(expert_ids.shape[::-1], expert_ids.dtype),
            pltpu.VMEM(expert_gates.shape[::-1], F32),
            pltpu.VMEM((2 * queries.shape[1] // HD * rows, HD), F32),
            pltpu.SemaphoreType.DMA((6 + len(later),)),
        ],
    )
    parts = exchange(parts, "seq")
    cost = pl.CostEstimate(flops=1 << 33, bytes_accessed=1 << 25, transcendentals=0)
    (joined,) = call(combine, [((seq * SLOTS, LANES), BF16)], [parts], cost=cost)
    joined = exchange(joined, "seq")
    (chosen,) = call(
        project,
        [((head * seq * 2, LANES), BF16)],
        [joined, weight, residual, pick],
        scratch=[pltpu.VMEM((seq * SLOTS, LANES), F32)],
        cost=cost,
    )
    chosen = exchange(chosen, ("head", "seq"))
    (outputs,) = call(
        experts,
        [((head * seq * 2, LANES), BF16)],
        [chosen, gain, gate_weight, up_weight, down_weight, route],
    )
    outputs = exchange(outputs, ("head", "seq"))
    return call(
        finish,
        [(residual.shape, BF16), ((rows, residual.shape[1] // head), BF16)],
        [outputs, turned],
        results=(0, 1),
    )


def solution(mesh):
    in_specs = (
        P(None, "head"),
        P(None, "seq", "head"),
        P(None, "seq", "head"),
        P(),
        P(None, "seq"),
        P("head", "seq"),
        P(),
        P(),
        P(),
        P("seq", None, "head"),
        P("seq", None, "head"),
        P("seq", "head", None),
    )
    out_specs = (P(None, "seq"), P(None, ("seq", "head")))
    return jax.shard_map(local, mesh=mesh, in_specs=in_specs, out_specs=out_specs, check_vma=False)
```

```python
import math

import jax
import jax.numpy as jnp
from jax import lax
from jax.experimental import pallas as pl
from jax.experimental.pallas import tpu as pltpu
from jax.sharding import Mesh
from jax.sharding import PartitionSpec as P

HD = 128
LANES = 128
NEAR = 8
PAIRS = 32
PIECE = PAIRS + PAIRS // 4
MASKED = -1e30
F32 = jnp.float32
BF16 = jnp.bfloat16
NT = (((1,), (1,)), ((), ()))


def iota(shape, dim):
    return lax.broadcasted_iota(jnp.int32, shape, dim)


def call(body, outs, args, hbm=(), results=(), scratch=(), limit=16 << 20, cost=None):
    spaces = [pltpu.HBM if i in hbm else pltpu.VMEM for i in range(len(args))]
    args = [pltpu.with_memory_space_constraint(a, s) if s is pltpu.HBM else a for a, s in zip(args, spaces)]
    return pl.pallas_call(
        body,
        out_shape=[
            jax.ShapeDtypeStruct(shape, dtype) if i in results else pltpu.VMEM(shape, dtype)
            for i, (shape, dtype) in enumerate(outs)
        ],
        in_specs=[pl.BlockSpec(memory_space=s) for s in spaces],
        out_specs=[pl.BlockSpec(memory_space=pltpu.VMEM) for _ in outs],
        scratch_shapes=list(scratch),
        compiler_params=pltpu.CompilerParams(vmem_limit_bytes=limit),
        cost_estimate=cost,
    )(*args)


def attend(lengths_hbm, q_hbm, k_hbm, v_hbm, ids_hbm, gates_hbm, *refs):
    lengths, q, k, v, ids, gates, wide, sems = refs[-8:]
    later = (len(refs) - 12) // 2
    out, pick, turned, route = refs[2 * later : -8]
    rows, heads = q.shape[0], q.shape[1] // HD
    pairs = [(ids_hbm, ids), (gates_hbm, gates), (q_hbm, q), (k_hbm, k), (lengths_hbm, lengths), (v_hbm, v)]
    pairs += [(refs[i], refs[later + i]) for i in range(later)]
    fetch = [pltpu.make_async_copy(far, near, sems.at[i]) for i, (far, near) in enumerate(pairs)]
    for copy in fetch:
        copy.start()
    fetch[0].wait()
    fetch[1].wait()
    routing(ids[...], gates[...], pick, turned, route)
    fetch[2].wait()
    for h in range(heads):
        wide[pl.ds(h * rows, rows), :] = q[:, h * HD : (h + 1) * HD].astype(F32)
    fetch[3].wait()
    scores = [
        lax.dot_general(
            wide[pl.ds(r, heads, stride=rows), :].astype(BF16), k[r], NT, preferred_element_type=F32
        )
        for r in range(rows)
    ]
    scores = jnp.concatenate(scores, axis=0) * (1.0 / math.sqrt(HD))
    fetch[4].wait()
    place = own_block() * k.shape[1] + iota((heads, k.shape[1]), 1)
    valid = jnp.concatenate([place < lengths[r] for r in range(rows)], axis=0)
    top = jnp.max(jnp.where(valid, scores, MASKED), axis=1, keepdims=True).astype(BF16).astype(F32)
    weights = jnp.where(valid, jnp.exp(scores - top), 0.0).astype(BF16)
    total = jnp.sum(weights.astype(F32), axis=1, keepdims=True)
    fetch[5].wait()
    numer = [
        jnp.dot(weights[r * heads : (r + 1) * heads], v[r], preferred_element_type=F32)
        for r in range(rows)
    ]
    out[...] = joint(jnp.concatenate(numer, axis=0), top, total, out.shape[0] // PIECE)
    for copy in fetch[6:]:
        copy.wait()


def routing(ids, gates, pick, turned, route):
    chosen = selection(ids, pick.shape[0] // 2)
    pick[...] = chosen.astype(BF16)
    first = jnp.concatenate([ids[0:1, :], ids[0:1, :]], axis=1) == iota(chosen.shape, 0) // 2
    first = jnp.where(first, chosen, 0.0)
    both = jnp.concatenate([chosen, first, jnp.zeros((pick.shape[0], LANES - 2 * pick.shape[1]), F32)], axis=1)
    turned[...] = both.T[: turned.shape[0]].astype(BF16)

    rows = ids.shape[1]
    mine = ids == own_block()
    gate = jnp.sum(jnp.where(mine, gates, 0.0), axis=0, keepdims=True)
    here = jnp.broadcast_to(jnp.max(mine.astype(F32), axis=0, keepdims=True), (8, rows))
    before = (iota((rows, rows), 0) < iota((rows, rows), 1)).astype(F32)
    rank = jnp.dot(here, before, preferred_element_type=F32)
    taken = (rank == iota((8, rows), 0).astype(F32)) & (here > 0.0)
    weight = jnp.sum(jnp.where(taken, gate, 0.0), axis=1, keepdims=True)
    route[...] = jnp.broadcast_to(weight, route.shape)


def own_block():
    return lax.axis_index("far") * lax.axis_size("near") + lax.axis_index("near")


def joint(numer, top, total, count):
    pairs = numer.shape[0]
    lane, row = iota(numer.shape, 1), iota(numer.shape, 0)
    high = total.astype(BF16).astype(F32)
    part = lane % 32
    stats = jnp.where(part < 16, top, jnp.where(part < 24, high, total - high))
    stats = jnp.where(lane // 32 == row % 4, stats, 0.0).astype(BF16)
    gather = (iota((pairs // 4, pairs), 0) == iota((pairs // 4, pairs), 1) // 4).astype(BF16)
    packed = jnp.dot(gather, stats, preferred_element_type=F32)
    pieces = []
    for i in range(count):
        pieces += [numer[i * PAIRS : (i + 1) * PAIRS], packed[i * PAIRS // 4 : (i + 1) * PAIRS // 4]]
    return jnp.concatenate(pieces, axis=0).astype(BF16)


def merged(pieces):
    count = pieces.shape[0] // PIECE
    wide = pieces.astype(F32)
    parts = [wide[i * PIECE : (i + 1) * PIECE] for i in range(count)]
    numer = [part[:PAIRS] for part in parts]
    packed = jnp.concatenate([part[PAIRS:] for part in parts], axis=0).astype(BF16)
    pairs = count * PAIRS
    spread = (iota((pairs, pairs // 4), 0) // 4 == iota((pairs, pairs // 4), 1)).astype(BF16)
    stats = jnp.dot(spread, packed, preferred_element_type=F32)
    at = iota(stats.shape, 1) - 32 * (iota(stats.shape, 0) % 4)
    ones = jnp.ones((LANES, LANES), BF16)
    tops = jnp.dot(jnp.where(at == 0, stats, 0.0).astype(BF16), ones, preferred_element_type=F32)
    sums = jnp.where((at == 16) | (at == 24), stats, 0.0).astype(BF16)
    sums = jnp.dot(sums, ones, preferred_element_type=F32)
    top = tops[:PAIRS]
    for i in range(1, count):
        top = jnp.maximum(top, tops[i * PAIRS : (i + 1) * PAIRS])
    numers = totals = jnp.zeros((PAIRS, LANES), F32)
    for i in range(count):
        scale = jnp.exp(tops[i * PAIRS : (i + 1) * PAIRS] - top)
        numers = numers + scale * numer[i]
        totals = totals + scale * sums[i * PAIRS : (i + 1) * PAIRS]
    return numers, top, totals


def combine(parts, out):
    numer, top, total = merged(parts[...])
    piece = joint(numer, top, total, 1)
    out[...] = jnp.concatenate([piece.astype(F32)] * (out.shape[0] // PIECE), axis=0).astype(BF16)


def complete(parts, out):
    numer, _, total = merged(parts[...])
    out[...] = jnp.concatenate([(numer / total).astype(BF16)] * (out.shape[0] // PAIRS), axis=0)


def project(pieces, weight, residual, pick, out, wide):
    rows = residual.shape[0]
    heads = pieces.shape[0] // rows
    wide[...] = pieces[...].astype(F32)
    lhs = jnp.concatenate(
        [wide[pl.ds(h, rows, stride=heads), :].astype(BF16) for h in range(heads)], axis=1
    )
    part = lax.dot_general(lhs, weight[...], NT, preferred_element_type=F32)
    part = part + jnp.where(lax.axis_index("head") == 0, residual[...].astype(F32), 0.0)
    none = jnp.zeros_like(part)
    twice = jnp.concatenate(
        [jnp.concatenate([part, none], axis=1), jnp.concatenate([none, part], axis=1)], axis=0
    ).astype(BF16)
    send = jnp.dot(pick[...], twice, preferred_element_type=F32).astype(BF16)
    out[...] = jnp.concatenate([send] * (out.shape[0] // send.shape[0]), axis=0)


def selection(ids, count):
    top_k, rows = ids.shape
    shape = (count * 2, 2 * rows)
    expert = iota(shape, 0) // 2
    wide = jnp.concatenate([ids, ids], axis=1)
    hit = expert == wide[0:1, :]
    for k in range(1, top_k):
        hit = hit | (expert == wide[k : k + 1, :])
    hit = hit.astype(F32)
    square = (2 * rows, 2 * rows)
    before = (iota(square, 0) < iota(square, 1) % rows).astype(F32)
    rank = jnp.dot(hit, before, preferred_element_type=F32)
    slot = iota(shape, 0) % 2 + 2 * (iota(shape, 1) // rows)
    return jnp.where(rank == slot.astype(F32), hit, 0.0)


def swap(y):
    count = y.shape[0]
    row = iota(y.shape, 0) % 4
    lane = iota(y.shape, 1)
    z = pltpu.roll(y, 64, 1)
    up = pltpu.roll(z, count - 2, 0)
    down = pltpu.roll(z, 2, 0)
    return jnp.where(lane < 64, jnp.where(row < 2, y, down), jnp.where(row < 2, up, y))


def experts(pieces, gain, gate, up, down, route, out):
    width = gain.shape[1]
    blocks = width // LANES
    half = 2 * lax.axis_size("far") * lax.axis_size("near")
    heads = pieces.shape[0] // half
    summed = pieces[:half].astype(F32)
    for i in range(1, heads):
        summed = summed + pieces[i * half : (i + 1) * half].astype(F32)
    stacked = swap(summed).astype(BF16).astype(F32)
    tiles = []
    for b in range(blocks):
        tile = stacked[8 * (b // 2) : 8 * (b // 2) + 8]
        tiles.append(tile if b % 2 == 0 else pltpu.roll(tile, 4, 0))
    x = jnp.concatenate(tiles, axis=1)
    square = jnp.sum(x * x, axis=1, keepdims=True) * (1.0 / width)
    normed = (x * lax.rsqrt(square + 1e-6) * gain[...]).astype(BF16)
    gate_proj = jnp.dot(normed, gate[0], preferred_element_type=F32)
    up_proj = jnp.dot(normed, up[0], preferred_element_type=F32)
    hidden = (gate_proj / (1.0 + jnp.exp(-gate_proj)) * up_proj).astype(BF16)
    result = jnp.dot(hidden, down[0], preferred_element_type=F32) * route[:, 0:1]

    lower = iota((8, LANES), 0) < 4
    pairs = []
    for b in range(0, blocks, 2):
        left = result[:, b * LANES : (b + 1) * LANES]
        right = result[:, (b + 1) * LANES : (b + 2) * LANES]
        pairs.append(jnp.where(lower, left, pltpu.roll(right, 4, 0)))
    mixed = jnp.concatenate(pairs, axis=0)
    head = lax.axis_index("head")
    group = iota(mixed.shape, 1) // 16 % heads
    moved = pltpu.roll(stacked, jnp.where(head % 2 == 0, 16, LANES - 16), 1)
    for target in range(heads):
        carried = jnp.where(target == head, moved, stacked)
        packed = swap(jnp.where(group == target, mixed, carried))
        out[pl.ds(target * half, half), :] = packed.astype(BF16)


def finish(pieces, turned, after, out):
    half = turned.shape[1]
    rows, width = out.shape
    heads = pieces.shape[0] // half
    head = lax.axis_index("head")
    group = iota((rows, LANES), 1) // 16
    mixture = jnp.zeros((rows, LANES), F32)
    own = jnp.zeros((rows, LANES), F32)
    for source in range(heads):
        got = jnp.dot(turned[...], pieces[source * half : (source + 1) * half], preferred_element_type=F32)
        mixture = mixture + got[:rows] + pltpu.roll(got[rows : 2 * rows], 64, 1)
        carried = got[2 * rows : 3 * rows] + pltpu.roll(got[3 * rows :], 64, 1)
        moved = pltpu.roll(carried, LANES - 16 if source % 2 == 0 else 16, 1)
        own = own + jnp.where(group == source, jnp.where(head == source, moved, carried), 0.0)
    after[...] = own[:, : after.shape[1]].astype(BF16)
    shift = (LANES - width * head) % LANES
    out[...] = pltpu.roll(mixture + own, shift, 1)[:, :width].astype(BF16)


def exchange(x, axis):
    return lax.all_to_all(x, axis, 0, 0, tiled=True)


def local(
    queries,
    keys,
    values,
    lengths,
    residual,
    out_weight,
    norm_gain,
    expert_ids,
    expert_gates,
    gate_weight,
    up_weight,
    down_weight,
):
    far, near, head = lax.axis_size("far"), lax.axis_size("near"), lax.axis_size("head")
    seq = far * near
    rows = queries.shape[0]
    later = [out_weight.T, residual, norm_gain.reshape(1, -1)]
    weight, residual, gain, parts, pick, turned, route = call(
        attend,
        [(a.shape, a.dtype) for a in later]
        + [((near * PIECE, LANES), BF16)]
        + [((seq * 2, 2 * rows), BF16), ((4 * rows, seq * 2), BF16), ((8, LANES), F32)],
        [lengths, queries, keys, values, expert_ids.T, expert_gates.T, *later],
        hbm=range(6 + len(later)),
        scratch=[
            pltpu.SMEM(lengths.shape, lengths.dtype),
            pltpu.VMEM(queries.shape, BF16),
            pltpu.VMEM(keys.shape, BF16),
            pltpu.VMEM(values.shape, BF16),
            pltpu.VMEM(expert_ids.shape[::-1], expert_ids.dtype),
            pltpu.VMEM(expert_gates.shape[::-1], F32),
            pltpu.VMEM((queries.shape[1] // HD * rows, HD), F32),
            pltpu.SemaphoreType.DMA((6 + len(later),)),
        ],
    )
    parts = exchange(parts, "near")
    cost = pl.CostEstimate(flops=1 << 33, bytes_accessed=1 << 25, transcendentals=0)
    (parts,) = call(combine, [((far * PIECE, LANES), BF16)], [parts], cost=cost)
    parts = exchange(parts, "far")
    (joined,) = call(complete, [((near * PAIRS, LANES), BF16)], [parts], cost=cost)
    joined = exchange(joined, "near")
    (chosen,) = call(
        project,
        [((head * seq * 2, LANES), BF16)],
        [joined, weight, residual, pick],
        scratch=[pltpu.VMEM((near * PAIRS, LANES), F32)],
        cost=cost,
    )
    chosen = exchange(chosen, ("head", "far", "near"))
    (outputs,) = call(
        experts,
        [((head * seq * 2, LANES), BF16)],
        [chosen, gain, gate_weight, up_weight, down_weight, route],
    )
    outputs = exchange(outputs, ("head", "far", "near"))
    return call(
        finish,
        [(residual.shape, BF16), ((rows, residual.shape[1] // head), BF16)],
        [outputs, turned],
        results=(0, 1),
    )


def solution(mesh):
    seq, head = mesh.shape["seq"], mesh.shape["head"]
    mesh = Mesh(mesh.devices.reshape(seq // NEAR, NEAR, head), ("far", "near", "head"))
    seq = ("far", "near")
    in_specs = (
        P(None, "head"),
        P(None, seq, "head"),
        P(None, seq, "head"),
        P(),
        P(None, seq),
        P("head", seq),
        P(),
        P(),
        P(),
        P(seq, None, "head"),
        P(seq, None, "head"),
        P(seq, "head", None),
    )
    out_specs = (P(None, seq), P(None, (*seq, "head")))
    return jax.shard_map(local, mesh=mesh, in_specs=in_specs, out_specs=out_specs, check_vma=False)
```

```python
import math

import jax
import jax.numpy as jnp
from jax import lax
from jax.experimental import pallas as pl
from jax.experimental.pallas import tpu as pltpu
from jax.sharding import Mesh
from jax.sharding import PartitionSpec as P

HD = 128
LANES = 128
NEAR = 8
PAIRS = 32
PIECE = PAIRS + PAIRS // 4
MASKED = -1e30
F32 = jnp.float32
BF16 = jnp.bfloat16
NT = (((1,), (1,)), ((), ()))


def iota(shape, dim):
    return lax.broadcasted_iota(jnp.int32, shape, dim)


def call(body, outs, args, hbm=(), results=(), scratch=(), limit=16 << 20, cost=None):
    spaces = [pltpu.HBM if i in hbm else pltpu.VMEM for i in range(len(args))]
    args = [pltpu.with_memory_space_constraint(a, s) if s is pltpu.HBM else a for a, s in zip(args, spaces)]
    return pl.pallas_call(
        body,
        out_shape=[
            jax.ShapeDtypeStruct(shape, dtype) if i in results else pltpu.VMEM(shape, dtype)
            for i, (shape, dtype) in enumerate(outs)
        ],
        in_specs=[pl.BlockSpec(memory_space=s) for s in spaces],
        out_specs=[pl.BlockSpec(memory_space=pltpu.VMEM) for _ in outs],
        scratch_shapes=list(scratch),
        compiler_params=pltpu.CompilerParams(vmem_limit_bytes=limit),
        cost_estimate=cost,
    )(*args)


def attend(lengths_hbm, q_hbm, k_hbm, v_hbm, ids_hbm, gates_hbm, *refs):
    lengths, q, k, v, ids, gates, wide, sems = refs[-8:]
    later = (len(refs) - 12) // 2
    out, pick, turned, route = refs[2 * later : -8]
    rows, heads = q.shape[0], q.shape[1] // HD
    pairs = [(ids_hbm, ids), (gates_hbm, gates), (q_hbm, q), (k_hbm, k), (lengths_hbm, lengths), (v_hbm, v)]
    pairs += [(refs[i], refs[later + i]) for i in range(later)]
    fetch = [pltpu.make_async_copy(far, near, sems.at[i]) for i, (far, near) in enumerate(pairs)]
    for copy in fetch:
        copy.start()
    fetch[0].wait()
    fetch[1].wait()
    routing(ids[...], gates[...], pick, turned, route)
    fetch[2].wait()
    for h in range(heads):
        wide[pl.ds(h * rows, rows), :] = q[:, h * HD : (h + 1) * HD].astype(F32)
    fetch[3].wait()
    scores = [
        lax.dot_general(
            wide[pl.ds(r, heads, stride=rows), :].astype(BF16), k[r], NT, preferred_element_type=F32
        )
        for r in range(rows)
    ]
    scores = jnp.concatenate(scores, axis=0) * (1.0 / math.sqrt(HD))
    fetch[4].wait()
    place = own_block() * k.shape[1] + iota((heads, k.shape[1]), 1)
    valid = jnp.concatenate([place < lengths[r] for r in range(rows)], axis=0)
    top = jnp.max(jnp.where(valid, scores, MASKED), axis=1, keepdims=True).astype(BF16).astype(F32)
    weights = jnp.where(valid, jnp.exp(scores - top), 0.0).astype(BF16)
    total = jnp.sum(weights.astype(F32), axis=1, keepdims=True)
    fetch[5].wait()
    numer = [
        jnp.dot(weights[r * heads : (r + 1) * heads], v[r], preferred_element_type=F32)
        for r in range(rows)
    ]
    out[...] = joint(jnp.concatenate(numer, axis=0), top, total, out.shape[0] // PIECE)
    for copy in fetch[6:]:
        copy.wait()


def routing(ids, gates, pick, turned, route):
    chosen = selection(ids, pick.shape[0] // 2)
    pick[...] = chosen.astype(BF16)
    first = jnp.concatenate([ids[0:1, :], ids[0:1, :]], axis=1) == iota(chosen.shape, 0) // 2
    first = jnp.where(first, chosen, 0.0)
    both = jnp.concatenate([chosen, first, jnp.zeros((pick.shape[0], LANES - 2 * pick.shape[1]), F32)], axis=1)
    turned[...] = both.T[: turned.shape[0]].astype(BF16)

    rows = ids.shape[1]
    mine = ids == own_block()
    gate = jnp.sum(jnp.where(mine, gates, 0.0), axis=0, keepdims=True)
    here = jnp.broadcast_to(jnp.max(mine.astype(F32), axis=0, keepdims=True), (8, rows))
    before = (iota((rows, rows), 0) < iota((rows, rows), 1)).astype(F32)
    rank = jnp.dot(here, before, preferred_element_type=F32)
    taken = (rank == iota((8, rows), 0).astype(F32)) & (here > 0.0)
    weight = jnp.sum(jnp.where(taken, gate, 0.0), axis=1, keepdims=True)
    route[...] = jnp.broadcast_to(weight, route.shape)


def own_block():
    return lax.axis_index("far") * lax.axis_size("near") + lax.axis_index("near")


def joint(numer, top, total, count):
    lane = iota(numer.shape, 1)
    high = total.astype(BF16).astype(F32)
    part = lane % 32
    stats = jnp.where(part < 16, top, jnp.where(part < 24, high, total - high))
    lane = iota((8, LANES), 1)
    pieces = []
    for i in range(count):
        quarters = [stats[i * PAIRS + 8 * a : i * PAIRS + 8 * a + 8] for a in range(PAIRS // 8)]
        packed = quarters[-1]
        for a in range(PAIRS // 8 - 1):
            packed = jnp.where(lane // 32 == a, quarters[a], packed)
        pieces += [numer[i * PAIRS : (i + 1) * PAIRS], packed]
    return jnp.concatenate(pieces, axis=0).astype(BF16)


def merged(pieces):
    wide = pieces.astype(F32)
    parts = [wide[i : i + PIECE] for i in range(0, pieces.shape[0], PIECE)]
    packed = [part[PAIRS:] for part in parts]
    top = packed[0]
    for one in packed[1:]:
        top = jnp.maximum(top, one)
    numers, totals = jnp.zeros((PAIRS, LANES), F32), jnp.zeros((8, LANES), F32)
    for part, one in zip(parts, packed):
        scale = jnp.exp(one - top)
        totals = totals + pltpu.roll(scale, 16, 1) * one
        column = jnp.concatenate(
            [jnp.broadcast_to(scale[:, a : a + 1], (8, LANES)) for a in range(0, LANES, 32)], axis=0
        )
        numers = numers + column * part[:PAIRS]
    return numers, top, totals + pltpu.roll(totals, LANES - 8, 1)


def combine(parts, out):
    numer, top, total = merged(parts[...])
    part = iota(top.shape, 1) % 32
    high = total.astype(BF16).astype(F32)
    packed = jnp.where(part < 16, top, jnp.where(part < 24, high, pltpu.roll(total - high, 8, 1)))
    out[...] = jnp.concatenate([numer, packed] * (out.shape[0] // PIECE), axis=0).astype(BF16)


def complete(parts, out):
    numer, _, total = merged(parts[...])
    column = jnp.concatenate(
        [jnp.broadcast_to(total[:, a : a + 1], (8, LANES)) for a in range(16, LANES, 32)], axis=0
    )
    out[...] = jnp.concatenate([(numer / column).astype(BF16)] * (out.shape[0] // PAIRS), axis=0)


def project(pieces, weight, residual, pick, out, wide):
    rows = residual.shape[0]
    heads = pieces.shape[0] // rows
    wide[...] = pieces[...].astype(F32)
    lhs = jnp.concatenate(
        [wide[pl.ds(h, rows, stride=heads), :].astype(BF16) for h in range(heads)], axis=1
    )
    part = lax.dot_general(lhs, weight[...], NT, preferred_element_type=F32)
    part = part + jnp.where(lax.axis_index("head") == 0, residual[...].astype(F32), 0.0)
    none = jnp.zeros_like(part)
    twice = jnp.concatenate(
        [jnp.concatenate([part, none], axis=1), jnp.concatenate([none, part], axis=1)], axis=0
    ).astype(BF16)
    send = jnp.dot(pick[...], twice, preferred_element_type=F32).astype(BF16)
    out[...] = jnp.concatenate([send] * (out.shape[0] // send.shape[0]), axis=0)


def selection(ids, count):
    top_k, rows = ids.shape
    shape = (count * 2, 2 * rows)
    expert = iota(shape, 0) // 2
    wide = jnp.concatenate([ids, ids], axis=1)
    hit = expert == wide[0:1, :]
    for k in range(1, top_k):
        hit = hit | (expert == wide[k : k + 1, :])
    hit = hit.astype(F32)
    square = (2 * rows, 2 * rows)
    before = (iota(square, 0) < iota(square, 1) % rows).astype(F32)
    rank = jnp.dot(hit, before, preferred_element_type=F32)
    slot = iota(shape, 0) % 2 + 2 * (iota(shape, 1) // rows)
    return jnp.where(rank == slot.astype(F32), hit, 0.0)


def swap(y):
    count = y.shape[0]
    row = iota(y.shape, 0) % 4
    lane = iota(y.shape, 1)
    z = pltpu.roll(y, 64, 1)
    up = pltpu.roll(z, count - 2, 0)
    down = pltpu.roll(z, 2, 0)
    return jnp.where(lane < 64, jnp.where(row < 2, y, down), jnp.where(row < 2, up, y))


def experts(pieces, gain, gate, up, down, route, out):
    width = gain.shape[1]
    blocks = width // LANES
    half = 2 * lax.axis_size("far") * lax.axis_size("near")
    heads = pieces.shape[0] // half
    summed = pieces[:half].astype(F32)
    for i in range(1, heads):
        summed = summed + pieces[i * half : (i + 1) * half].astype(F32)
    stacked = swap(summed).astype(BF16).astype(F32)
    tiles = []
    for b in range(blocks):
        tile = stacked[8 * (b // 2) : 8 * (b // 2) + 8]
        tiles.append(tile if b % 2 == 0 else pltpu.roll(tile, 4, 0))
    x = jnp.concatenate(tiles, axis=1)
    square = jnp.sum(x * x, axis=1, keepdims=True) * (1.0 / width)
    normed = (x * lax.rsqrt(square + 1e-6) * gain[...]).astype(BF16)
    gate_proj = jnp.dot(normed, gate[0], preferred_element_type=F32)
    up_proj = jnp.dot(normed, up[0], preferred_element_type=F32)
    hidden = (gate_proj / (1.0 + jnp.exp(-gate_proj)) * up_proj).astype(BF16)
    result = jnp.dot(hidden, down[0], preferred_element_type=F32) * route[:, 0:1]

    lower = iota((8, LANES), 0) < 4
    pairs = []
    for b in range(0, blocks, 2):
        left = result[:, b * LANES : (b + 1) * LANES]
        right = result[:, (b + 1) * LANES : (b + 2) * LANES]
        pairs.append(jnp.where(lower, left, pltpu.roll(right, 4, 0)))
    mixed = jnp.concatenate(pairs, axis=0)
    head = lax.axis_index("head")
    group = iota(mixed.shape, 1) // 16 % heads
    moved = pltpu.roll(stacked, jnp.where(head % 2 == 0, 16, LANES - 16), 1)
    for target in range(heads):
        carried = jnp.where(target == head, moved, stacked)
        packed = swap(jnp.where(group == target, mixed, carried))
        out[pl.ds(target * half, half), :] = packed.astype(BF16)


def finish(pieces, turned, after, out):
    half = turned.shape[1]
    rows, width = out.shape
    heads = pieces.shape[0] // half
    head = lax.axis_index("head")
    group = iota((rows, LANES), 1) // 16 % heads
    none = jnp.zeros((rows, LANES), F32)
    mixture, own, beside = [none, none], [none, none], [none, none]
    for source in range(heads):
        got = jnp.dot(turned[...], pieces[source * half : (source + 1) * half], preferred_element_type=F32)
        here = (group == source) & (head != source)
        next_to = (group == source ^ 1) & (head == source)
        for i in range(2):
            carried = got[(2 + i) * rows : (3 + i) * rows]
            mixture[i] = mixture[i] + got[i * rows : (i + 1) * rows]
            own[i] = own[i] + jnp.where(here, carried, 0.0)
            beside[i] = beside[i] + jnp.where(next_to, carried, 0.0)
    mixture, own, beside = [left + pltpu.roll(right, 64, 1) for left, right in (mixture, own, beside)]
    own = own + pltpu.roll(beside, jnp.where(head % 2 == 0, LANES - 16, 16), 1)
    after[...] = own[:, : after.shape[1]].astype(BF16)
    shift = (LANES - width * head) % LANES
    out[...] = pltpu.roll(mixture + own, shift, 1)[:, :width].astype(BF16)


def exchange(x, axis):
    return lax.all_to_all(x, axis, 0, 0, tiled=True)


def local(
    queries,
    keys,
    values,
    lengths,
    residual,
    out_weight,
    norm_gain,
    expert_ids,
    expert_gates,
    gate_weight,
    up_weight,
    down_weight,
):
    far, near, head = lax.axis_size("far"), lax.axis_size("near"), lax.axis_size("head")
    seq = far * near
    rows = queries.shape[0]
    later = [out_weight.T, residual, norm_gain.reshape(1, -1)]
    weight, residual, gain, parts, pick, turned, route = call(
        attend,
        [(a.shape, a.dtype) for a in later]
        + [((near * PIECE, LANES), BF16)]
        + [((seq * 2, 2 * rows), BF16), ((4 * rows, seq * 2), BF16), ((8, LANES), F32)],
        [lengths, queries, keys, values, expert_ids.T, expert_gates.T, *later],
        hbm=range(6 + len(later)),
        scratch=[
            pltpu.SMEM(lengths.shape, lengths.dtype),
            pltpu.VMEM(queries.shape, BF16),
            pltpu.VMEM(keys.shape, BF16),
            pltpu.VMEM(values.shape, BF16),
            pltpu.VMEM(expert_ids.shape[::-1], expert_ids.dtype),
            pltpu.VMEM(expert_gates.shape[::-1], F32),
            pltpu.VMEM((queries.shape[1] // HD * rows, HD), F32),
            pltpu.SemaphoreType.DMA((6 + len(later),)),
        ],
    )
    parts = exchange(parts, "near")
    cost = pl.CostEstimate(flops=1 << 33, bytes_accessed=1 << 25, transcendentals=0)
    (parts,) = call(combine, [((far * PIECE, LANES), BF16)], [parts], cost=cost)
    parts = exchange(parts, "far")
    (joined,) = call(complete, [((near * PAIRS, LANES), BF16)], [parts], cost=cost)
    joined = exchange(joined, "near")
    (chosen,) = call(
        project,
        [((head * seq * 2, LANES), BF16)],
        [joined, weight, residual, pick],
        scratch=[pltpu.VMEM((near * PAIRS, LANES), F32)],
        cost=cost,
    )
    chosen = exchange(chosen, ("head", "far", "near"))
    (outputs,) = call(
        experts,
        [((head * seq * 2, LANES), BF16)],
        [chosen, gain, gate_weight, up_weight, down_weight, route],
    )
    outputs = exchange(outputs, ("head", "far", "near"))
    return call(
        finish,
        [(residual.shape, BF16), ((rows, residual.shape[1] // head), BF16)],
        [outputs, turned],
        results=(0, 1),
    )


def solution(mesh):
    seq, head = mesh.shape["seq"], mesh.shape["head"]
    mesh = Mesh(mesh.devices.reshape(seq // NEAR, NEAR, head), ("far", "near", "head"))
    seq = ("far", "near")
    in_specs = (
        P(None, "head"),
        P(None, seq, "head"),
        P(None, seq, "head"),
        P(),
        P(None, seq),
        P("head", seq),
        P(),
        P(),
        P(),
        P(seq, None, "head"),
        P(seq, None, "head"),
        P(seq, "head", None),
    )
    out_specs = (P(None, seq), P(None, (*seq, "head")))
    return jax.shard_map(local, mesh=mesh, in_specs=in_specs, out_specs=out_specs, check_vma=False)
```

```python
import math

import jax
import jax.numpy as jnp
from jax import lax
from jax.experimental import pallas as pl
from jax.experimental.pallas import tpu as pltpu
from jax.sharding import Mesh
from jax.sharding import PartitionSpec as P

HD = 128
LANES = 128
NEAR = 8
PAIRS = 32
PIECE = PAIRS + PAIRS // 4
MASKED = -1e30
F32 = jnp.float32
BF16 = jnp.bfloat16
NT = (((1,), (1,)), ((), ()))


def iota(shape, dim):
    return lax.broadcasted_iota(jnp.int32, shape, dim)


def call(body, outs, args, hbm=(), results=(), scratch=(), limit=16 << 20, cost=None):
    spaces = [pltpu.HBM if i in hbm else pltpu.VMEM for i in range(len(args))]
    args = [pltpu.with_memory_space_constraint(a, s) if s is pltpu.HBM else a for a, s in zip(args, spaces)]
    return pl.pallas_call(
        body,
        out_shape=[
            jax.ShapeDtypeStruct(shape, dtype) if i in results else pltpu.VMEM(shape, dtype)
            for i, (shape, dtype) in enumerate(outs)
        ],
        in_specs=[pl.BlockSpec(memory_space=s) for s in spaces],
        out_specs=[pl.BlockSpec(memory_space=pltpu.VMEM) for _ in outs],
        scratch_shapes=list(scratch),
        compiler_params=pltpu.CompilerParams(vmem_limit_bytes=limit),
        cost_estimate=cost,
    )(*args)


def attend(lengths_hbm, q_hbm, k_hbm, v_hbm, ids_hbm, gates_hbm, *refs):
    lengths, q, k, v, ids, gates, wide, sems = refs[-8:]
    later = (len(refs) - 12) // 2
    out, pick, turned, route = refs[2 * later : -8]
    rows, heads = q.shape[0], q.shape[1] // HD
    pairs = [(ids_hbm, ids), (gates_hbm, gates), (q_hbm, q), (k_hbm, k), (lengths_hbm, lengths), (v_hbm, v)]
    pairs += [(refs[i], refs[later + i]) for i in range(later)]
    fetch = [pltpu.make_async_copy(far, near, sems.at[i]) for i, (far, near) in enumerate(pairs)]
    for copy in fetch:
        copy.start()
    fetch[0].wait()
    fetch[1].wait()
    routing(ids[...], gates[...], pick, turned, route)
    for copy in fetch[2:6]:
        copy.wait()
    for h in range(heads):
        wide[pl.ds(h * rows, rows), :] = q[:, h * HD : (h + 1) * HD].astype(F32)
    scores = [
        lax.dot_general(
            wide[pl.ds(r, heads, stride=rows), :].astype(BF16), k[r], NT, preferred_element_type=F32
        )
        for r in range(rows)
    ]
    scores = jnp.concatenate(scores, axis=0) * (1.0 / math.sqrt(HD))
    place = own_block() * k.shape[1] + iota((heads, k.shape[1]), 1)
    valid = jnp.concatenate([place < lengths[r] for r in range(rows)], axis=0)
    top = jnp.max(jnp.where(valid, scores, MASKED), axis=1, keepdims=True).astype(BF16).astype(F32)
    weights = jnp.where(valid, jnp.exp(scores - top), 0.0).astype(BF16)
    total = jnp.sum(weights.astype(F32), axis=1, keepdims=True)
    numer = [
        jnp.dot(weights[r * heads : (r + 1) * heads], v[r], preferred_element_type=F32)
        for r in range(rows)
    ]
    out[...] = joint(jnp.concatenate(numer, axis=0), top, total, out.shape[0] // PIECE)
    for copy in fetch[6:]:
        copy.wait()


def routing(ids, gates, pick, turned, route):
    chosen = selection(ids, pick.shape[0] // 2)
    pick[...] = chosen.astype(BF16)
    first = jnp.concatenate([ids[0:1, :], ids[0:1, :]], axis=1) == iota(chosen.shape, 0) // 2
    first = jnp.where(first, chosen, 0.0)
    both = jnp.concatenate([chosen, first, jnp.zeros((pick.shape[0], LANES - 2 * pick.shape[1]), F32)], axis=1)
    turned[...] = both.T[: turned.shape[0]].astype(BF16)

    rows = ids.shape[1]
    mine = ids == own_block()
    gate = jnp.sum(jnp.where(mine, gates, 0.0), axis=0, keepdims=True)
    here = jnp.broadcast_to(jnp.max(mine.astype(F32), axis=0, keepdims=True), (8, rows))
    before = (iota((rows, rows), 0) < iota((rows, rows), 1)).astype(F32)
    rank = jnp.dot(here, before, preferred_element_type=F32)
    taken = (rank == iota((8, rows), 0).astype(F32)) & (here > 0.0)
    weight = jnp.sum(jnp.where(taken, gate, 0.0), axis=1, keepdims=True)
    route[...] = jnp.broadcast_to(weight, route.shape)


def own_block():
    return lax.axis_index("far") * lax.axis_size("near") + lax.axis_index("near")


def joint(numer, top, total, count):
    lane = iota(numer.shape, 1)
    high = total.astype(BF16).astype(F32)
    part = lane % 32
    stats = jnp.where(part < 16, top, jnp.where(part < 24, high, total - high))
    lane = iota((8, LANES), 1)
    pieces = []
    for i in range(count):
        quarters = [stats[i * PAIRS + 8 * a : i * PAIRS + 8 * a + 8] for a in range(PAIRS // 8)]
        packed = quarters[-1]
        for a in range(PAIRS // 8 - 1):
            packed = jnp.where(lane // 32 == a, quarters[a], packed)
        pieces += [numer[i * PAIRS : (i + 1) * PAIRS], packed]
    return jnp.concatenate(pieces, axis=0).astype(BF16)


def merged(pieces):
    wide = pieces.astype(F32)
    parts = [wide[i : i + PIECE] for i in range(0, pieces.shape[0], PIECE)]
    packed = [part[PAIRS:] for part in parts]
    top = packed[0]
    for one in packed[1:]:
        top = jnp.maximum(top, one)
    numers, totals = jnp.zeros((PAIRS, LANES), F32), jnp.zeros((8, LANES), F32)
    for part, one in zip(parts, packed):
        scale = jnp.exp(one - top)
        totals = totals + pltpu.roll(scale, 16, 1) * one
        column = jnp.concatenate(
            [jnp.broadcast_to(scale[:, a : a + 1], (8, LANES)) for a in range(0, LANES, 32)], axis=0
        )
        numers = numers + column * part[:PAIRS]
    return numers, top, totals + pltpu.roll(totals, LANES - 8, 1)


def combine(parts, out):
    numer, top, total = merged(parts[...])
    part = iota(top.shape, 1) % 32
    high = total.astype(BF16).astype(F32)
    packed = jnp.where(part < 16, top, jnp.where(part < 24, high, pltpu.roll(total - high, 8, 1)))
    out[...] = jnp.concatenate([numer, packed] * (out.shape[0] // PIECE), axis=0).astype(BF16)


def complete(parts, out):
    numer, _, total = merged(parts[...])
    column = jnp.concatenate(
        [jnp.broadcast_to(total[:, a : a + 1], (8, LANES)) for a in range(16, LANES, 32)], axis=0
    )
    out[...] = jnp.concatenate([(numer / column).astype(BF16)] * (out.shape[0] // PAIRS), axis=0)


def project(pieces, weight, residual, pick, out, wide):
    rows = residual.shape[0]
    heads = pieces.shape[0] // rows
    wide[...] = pieces[...].astype(F32)
    lhs = jnp.concatenate(
        [wide[pl.ds(h, rows, stride=heads), :].astype(BF16) for h in range(heads)], axis=1
    )
    part = lax.dot_general(lhs, weight[...], NT, preferred_element_type=F32)
    part = part + jnp.where(lax.axis_index("head") == 0, residual[...].astype(F32), 0.0)
    none = jnp.zeros_like(part)
    twice = jnp.concatenate(
        [jnp.concatenate([part, none], axis=1), jnp.concatenate([none, part], axis=1)], axis=0
    ).astype(BF16)
    send = jnp.dot(pick[...], twice, preferred_element_type=F32).astype(BF16)
    out[...] = jnp.concatenate([send] * (out.shape[0] // send.shape[0]), axis=0)


def selection(ids, count):
    top_k, rows = ids.shape
    shape = (count * 2, 2 * rows)
    expert = iota(shape, 0) // 2
    wide = jnp.concatenate([ids, ids], axis=1)
    hit = expert == wide[0:1, :]
    for k in range(1, top_k):
        hit = hit | (expert == wide[k : k + 1, :])
    hit = hit.astype(F32)
    square = (2 * rows, 2 * rows)
    before = (iota(square, 0) < iota(square, 1) % rows).astype(F32)
    rank = jnp.dot(hit, before, preferred_element_type=F32)
    slot = iota(shape, 0) % 2 + 2 * (iota(shape, 1) // rows)
    return jnp.where(rank == slot.astype(F32), hit, 0.0)


def swap(y):
    count = y.shape[0]
    row = iota(y.shape, 0) % 4
    lane = iota(y.shape, 1)
    z = pltpu.roll(y, 64, 1)
    up = pltpu.roll(z, count - 2, 0)
    down = pltpu.roll(z, 2, 0)
    return jnp.where(lane < 64, jnp.where(row < 2, y, down), jnp.where(row < 2, up, y))


def experts(pieces, gain, gate, up, down, route, out):
    width = gain.shape[1]
    blocks = width // LANES
    half = 2 * lax.axis_size("far") * lax.axis_size("near")
    heads = pieces.shape[0] // half
    summed = pieces[:half].astype(F32)
    for i in range(1, heads):
        summed = summed + pieces[i * half : (i + 1) * half].astype(F32)
    summed = summed.astype(BF16).astype(F32)
    stacked = swap(summed)
    tiles = []
    for b in range(blocks):
        tile = stacked[8 * (b // 2) : 8 * (b // 2) + 8]
        tiles.append(tile if b % 2 == 0 else pltpu.roll(tile, 4, 0))
    x = jnp.concatenate(tiles, axis=1)
    square = jnp.sum(x * x, axis=1, keepdims=True) * (1.0 / width)
    normed = (x * lax.rsqrt(square + 1e-6) * gain[...]).astype(BF16)
    gate_proj = jnp.dot(normed, gate[0], preferred_element_type=F32)
    up_proj = jnp.dot(normed, up[0], preferred_element_type=F32)
    hidden = (gate_proj / (1.0 + jnp.exp(-gate_proj)) * up_proj).astype(BF16)
    result = jnp.dot(hidden, down[0], preferred_element_type=F32) * route[:, 0:1]

    lower = iota((8, LANES), 0) < 4
    pairs = []
    for b in range(0, blocks, 2):
        left = result[:, b * LANES : (b + 1) * LANES]
        right = result[:, (b + 1) * LANES : (b + 2) * LANES]
        pairs.append(jnp.where(lower, left, pltpu.roll(right, 4, 0)))
    mixed = swap(jnp.concatenate(pairs, axis=0))
    head = lax.axis_index("head")
    group = iota(mixed.shape, 1) // 16 % heads
    moved = pltpu.roll(summed, jnp.where(head % 2 == 0, 16, LANES - 16), 1)
    for target in range(heads):
        carried = jnp.where(target == head, moved, summed)
        out[pl.ds(target * half, half), :] = jnp.where(group == target, mixed, carried).astype(BF16)


def finish(pieces, turned, after, out):
    half = turned.shape[1]
    rows, width = out.shape
    heads = pieces.shape[0] // half
    head = lax.axis_index("head")
    group = iota((rows, LANES), 1) // 16 % heads
    none = jnp.zeros((rows, LANES), F32)
    mixture, own, beside = [none, none], [none, none], [none, none]
    for source in range(heads):
        got = jnp.dot(turned[...], pieces[source * half : (source + 1) * half], preferred_element_type=F32)
        here = (group == source) & (head != source)
        next_to = (group == source ^ 1) & (head == source)
        for i in range(2):
            carried = got[(2 + i) * rows : (3 + i) * rows]
            mixture[i] = mixture[i] + got[i * rows : (i + 1) * rows]
            own[i] = own[i] + jnp.where(here, carried, 0.0)
            beside[i] = beside[i] + jnp.where(next_to, carried, 0.0)
    mixture, own, beside = [left + pltpu.roll(right, 64, 1) for left, right in (mixture, own, beside)]
    own = own + pltpu.roll(beside, jnp.where(head % 2 == 0, LANES - 16, 16), 1)
    after[...] = own[:, : after.shape[1]].astype(BF16)
    shift = (LANES - width * head) % LANES
    out[...] = pltpu.roll(mixture + own, shift, 1)[:, :width].astype(BF16)


def exchange(x, axis):
    return lax.all_to_all(x, axis, 0, 0, tiled=True)


def local(
    queries,
    keys,
    values,
    lengths,
    residual,
    out_weight,
    norm_gain,
    expert_ids,
    expert_gates,
    gate_weight,
    up_weight,
    down_weight,
):
    far, near, head = lax.axis_size("far"), lax.axis_size("near"), lax.axis_size("head")
    seq = far * near
    rows = queries.shape[0]
    later = [out_weight.T, residual, norm_gain.reshape(1, -1)]
    weight, residual, gain, parts, pick, turned, route = call(
        attend,
        [(a.shape, a.dtype) for a in later]
        + [((near * PIECE, LANES), BF16)]
        + [((seq * 2, 2 * rows), BF16), ((4 * rows, seq * 2), BF16), ((8, LANES), F32)],
        [lengths, queries, keys, values, expert_ids.T, expert_gates.T, *later],
        hbm=range(6 + len(later)),
        scratch=[
            pltpu.SMEM(lengths.shape, lengths.dtype),
            pltpu.VMEM(queries.shape, BF16),
            pltpu.VMEM(keys.shape, BF16),
            pltpu.VMEM(values.shape, BF16),
            pltpu.VMEM(expert_ids.shape[::-1], expert_ids.dtype),
            pltpu.VMEM(expert_gates.shape[::-1], F32),
            pltpu.VMEM((queries.shape[1] // HD * rows, HD), F32),
            pltpu.SemaphoreType.DMA((6 + len(later),)),
        ],
    )
    parts = exchange(parts, "near")
    cost = pl.CostEstimate(flops=1 << 33, bytes_accessed=1 << 25, transcendentals=0)
    (parts,) = call(combine, [((far * PIECE, LANES), BF16)], [parts], cost=cost)
    parts = exchange(parts, "far")
    (joined,) = call(complete, [((near * PAIRS, LANES), BF16)], [parts], cost=cost)
    joined = exchange(joined, "near")
    (chosen,) = call(
        project,
        [((head * seq * 2, LANES), BF16)],
        [joined, weight, residual, pick],
        scratch=[pltpu.VMEM((near * PAIRS, LANES), F32)],
        cost=cost,
    )
    chosen = exchange(chosen, ("head", "far", "near"))
    (outputs,) = call(
        experts,
        [((head * seq * 2, LANES), BF16)],
        [chosen, gain, gate_weight, up_weight, down_weight, route],
    )
    outputs = exchange(outputs, ("head", "far", "near"))
    return call(
        finish,
        [(residual.shape, BF16), ((rows, residual.shape[1] // head), BF16)],
        [outputs, turned],
        results=(0, 1),
    )


def solution(mesh):
    seq, head = mesh.shape["seq"], mesh.shape["head"]
    mesh = Mesh(mesh.devices.reshape(seq // NEAR, NEAR, head), ("far", "near", "head"))
    seq = ("far", "near")
    in_specs = (
        P(None, "head"),
        P(None, seq, "head"),
        P(None, seq, "head"),
        P(),
        P(None, seq),
        P("head", seq),
        P(),
        P(),
        P(),
        P(seq, None, "head"),
        P(seq, None, "head"),
        P(seq, "head", None),
    )
    out_specs = (P(None, seq), P(None, (*seq, "head")))
    return jax.shard_map(local, mesh=mesh, in_specs=in_specs, out_specs=out_specs, check_vma=False)
```

```python
import math

import jax
import jax.numpy as jnp
from jax import lax
from jax.experimental import pallas as pl
from jax.experimental.pallas import tpu as pltpu
from jax.sharding import Mesh
from jax.sharding import PartitionSpec as P

HD = 128
LANES = 128
NEAR = 8
PAIRS = 32
PIECE = PAIRS + PAIRS // 4
MASKED = -1e30
F32 = jnp.float32
BF16 = jnp.bfloat16
NT = (((1,), (1,)), ((), ()))


def iota(shape, dim):
    return lax.broadcasted_iota(jnp.int32, shape, dim)


def call(body, outs, args, hbm=(), results=(), scratch=(), limit=16 << 20, cost=None):
    spaces = [pltpu.HBM if i in hbm else pltpu.VMEM for i in range(len(args))]
    args = [pltpu.with_memory_space_constraint(a, s) if s is pltpu.HBM else a for a, s in zip(args, spaces)]
    return pl.pallas_call(
        body,
        out_shape=[
            jax.ShapeDtypeStruct(shape, dtype) if i in results else pltpu.VMEM(shape, dtype)
            for i, (shape, dtype) in enumerate(outs)
        ],
        in_specs=[pl.BlockSpec(memory_space=s) for s in spaces],
        out_specs=[pl.BlockSpec(memory_space=pltpu.VMEM) for _ in outs],
        scratch_shapes=list(scratch),
        compiler_params=pltpu.CompilerParams(vmem_limit_bytes=limit),
        cost_estimate=cost,
    )(*args)


def attend(lengths_hbm, q_hbm, k_hbm, v_hbm, ids_hbm, gates_hbm, *refs):
    lengths, q, k, v, ids, gates, wide, sems = refs[-8:]
    later = (len(refs) - 12) // 2
    out, pick, turned, route = refs[2 * later : -8]
    rows, heads = q.shape[0], q.shape[1] // HD
    pairs = [(ids_hbm, ids), (gates_hbm, gates), (q_hbm, q), (k_hbm, k), (lengths_hbm, lengths), (v_hbm, v)]
    pairs += [(refs[i], refs[later + i]) for i in range(later)]
    fetch = [pltpu.make_async_copy(far, near, sems.at[i]) for i, (far, near) in enumerate(pairs)]
    for copy in fetch:
        copy.start()
    fetch[0].wait()
    fetch[1].wait()
    routing(ids[...], gates[...], pick, turned, route)
    for copy in fetch[2:6]:
        copy.wait()
    for h in range(heads):
        wide[pl.ds(h * rows, rows), :] = q[:, h * HD : (h + 1) * HD].astype(F32)
    scores = [
        lax.dot_general(
            wide[pl.ds(r, heads, stride=rows), :].astype(BF16), k[r], NT, preferred_element_type=F32
        )
        for r in range(rows)
    ]
    scores = jnp.concatenate(scores, axis=0) * (1.0 / math.sqrt(HD))
    place = own_block() * k.shape[1] + iota((heads, k.shape[1]), 1)
    valid = jnp.concatenate([place < lengths[r] for r in range(rows)], axis=0)
    top = jnp.max(jnp.where(valid, scores, MASKED), axis=1, keepdims=True).astype(BF16).astype(F32)
    weights = jnp.where(valid, jnp.exp(scores - top), 0.0).astype(BF16)
    total = jnp.sum(weights.astype(F32), axis=1, keepdims=True)
    numer = [
        jnp.dot(weights[r * heads : (r + 1) * heads], v[r], preferred_element_type=F32)
        for r in range(rows)
    ]
    out[...] = joint(jnp.concatenate(numer, axis=0), top, total, out.shape[0] // PIECE)
    for copy in fetch[6:]:
        copy.wait()


def routing(ids, gates, pick, turned, route):
    chosen = selection(ids, pick.shape[0] // 2)
    pick[...] = chosen.astype(BF16)
    first = jnp.concatenate([ids[0:1, :], ids[0:1, :]], axis=1) == iota(chosen.shape, 0) // 2
    first = jnp.where(first, chosen, 0.0)
    both = jnp.concatenate([chosen, first, jnp.zeros((pick.shape[0], LANES - 2 * pick.shape[1]), F32)], axis=1)
    turned[...] = both.T[: turned.shape[0]].astype(BF16)

    rows = ids.shape[1]
    mine = ids == own_block()
    gate = jnp.sum(jnp.where(mine, gates, 0.0), axis=0, keepdims=True)
    here = jnp.broadcast_to(jnp.max(mine.astype(F32), axis=0, keepdims=True), (8, rows))
    before = (iota((rows, rows), 0) < iota((rows, rows), 1)).astype(F32)
    rank = jnp.dot(here, before, preferred_element_type=F32)
    taken = (rank == iota((8, rows), 0).astype(F32)) & (here > 0.0)
    weight = jnp.sum(jnp.where(taken, gate, 0.0), axis=1, keepdims=True)
    route[...] = jnp.broadcast_to(weight, route.shape)


def own_block():
    return lax.axis_index("far") * lax.axis_size("near") + lax.axis_index("near")


def joint(numer, top, total, count):
    lane = iota(numer.shape, 1)
    high = total.astype(BF16).astype(F32)
    part = lane % 32
    stats = jnp.where(part < 16, top, jnp.where(part < 24, high, total - high))
    lane = iota((8, LANES), 1)
    pieces = []
    for i in range(count):
        quarters = [stats[i * PAIRS + 8 * a : i * PAIRS + 8 * a + 8] for a in range(PAIRS // 8)]
        packed = quarters[-1]
        for a in range(PAIRS // 8 - 1):
            packed = jnp.where(lane // 32 == a, quarters[a], packed)
        pieces += [numer[i * PAIRS : (i + 1) * PAIRS], packed]
    return jnp.concatenate(pieces, axis=0).astype(BF16)


def merged(pieces):
    wide = pieces.astype(F32)
    parts = [wide[i : i + PIECE] for i in range(0, pieces.shape[0], PIECE)]
    packed = [part[PAIRS:] for part in parts]
    top = packed[0]
    for one in packed[1:]:
        top = jnp.maximum(top, one)
    numers, totals = jnp.zeros((PAIRS, LANES), F32), jnp.zeros((8, LANES), F32)
    for part, one in zip(parts, packed):
        scale = jnp.exp(one - top)
        totals = totals + pltpu.roll(scale, 16, 1) * one
        column = jnp.concatenate(
            [jnp.broadcast_to(scale[:, a : a + 1], (8, LANES)) for a in range(0, LANES, 32)], axis=0
        )
        numers = numers + column * part[:PAIRS]
    return numers, top, totals + pltpu.roll(totals, LANES - 8, 1)


def combine(parts, out):
    numer, top, total = merged(parts[...])
    part = iota(top.shape, 1) % 32
    high = total.astype(BF16).astype(F32)
    packed = jnp.where(part < 16, top, jnp.where(part < 24, high, pltpu.roll(total - high, 8, 1)))
    out[...] = jnp.concatenate([numer, packed] * (out.shape[0] // PIECE), axis=0).astype(BF16)


def complete(parts, out):
    numer, _, total = merged(parts[...])
    column = jnp.concatenate(
        [jnp.broadcast_to(total[:, a : a + 1], (8, LANES)) for a in range(16, LANES, 32)], axis=0
    )
    out[...] = jnp.concatenate([(numer / column).astype(BF16)] * (out.shape[0] // PAIRS), axis=0)


def project(pieces, weight, residual, pick, out, wide):
    rows = residual.shape[0]
    heads = pieces.shape[0] // rows
    wide[...] = pieces[...].astype(F32)
    lhs = jnp.concatenate(
        [wide[pl.ds(h, rows, stride=heads), :].astype(BF16) for h in range(heads)], axis=1
    )
    part = lax.dot_general(lhs, weight[...], NT, preferred_element_type=F32)
    part = part + jnp.where(lax.axis_index("head") == 0, residual[...].astype(F32), 0.0)
    none = jnp.zeros_like(part)
    twice = jnp.concatenate(
        [jnp.concatenate([part, none], axis=1), jnp.concatenate([none, part], axis=1)], axis=0
    ).astype(BF16)
    send = jnp.dot(pick[...], twice, preferred_element_type=F32).astype(BF16)
    out[...] = jnp.concatenate([send] * (out.shape[0] // send.shape[0]), axis=0)


def selection(ids, count):
    top_k, rows = ids.shape
    shape = (count * 2, 2 * rows)
    expert = iota(shape, 0) // 2
    wide = jnp.concatenate([ids, ids], axis=1)
    hit = expert == wide[0:1, :]
    for k in range(1, top_k):
        hit = hit | (expert == wide[k : k + 1, :])
    hit = hit.astype(F32)
    square = (2 * rows, 2 * rows)
    before = (iota(square, 0) < iota(square, 1) % rows).astype(F32)
    rank = jnp.dot(hit, before, preferred_element_type=F32)
    slot = iota(shape, 0) % 2 + 2 * (iota(shape, 1) // rows)
    return jnp.where(rank == slot.astype(F32), hit, 0.0)


def swap(y):
    count = y.shape[0]
    row = iota(y.shape, 0) % 4
    lane = iota(y.shape, 1)
    z = pltpu.roll(y, 64, 1)
    up = pltpu.roll(z, count - 2, 0)
    down = pltpu.roll(z, 2, 0)
    return jnp.where(lane < 64, jnp.where(row < 2, y, down), jnp.where(row < 2, up, y))


def experts(pieces, gain, gate, up, down, route, out):
    width = gain.shape[1]
    blocks = width // LANES
    half = 2 * lax.axis_size("far") * lax.axis_size("near")
    heads = pieces.shape[0] // half
    summed = pieces[:half].astype(F32)
    for i in range(1, heads):
        summed = summed + pieces[i * half : (i + 1) * half].astype(F32)
    summed = summed.astype(BF16).astype(F32)
    stacked = swap(summed)
    tiles = []
    for b in range(blocks):
        tile = stacked[8 * (b // 2) : 8 * (b // 2) + 8]
        tiles.append(tile if b % 2 == 0 else pltpu.roll(tile, 4, 0))
    x = jnp.concatenate(tiles, axis=1)
    square = jnp.sum(x * x, axis=1, keepdims=True) * (1.0 / width)
    scale = lax.rsqrt(square + 1e-6)
    scaled = (x * gain[...]).astype(BF16)
    gate_proj = jnp.dot(scaled, gate[0], preferred_element_type=F32) * scale
    up_proj = jnp.dot(scaled, up[0], preferred_element_type=F32) * scale
    hidden = (gate_proj / (1.0 + jnp.exp(-gate_proj)) * up_proj).astype(BF16)
    result = jnp.dot(hidden, down[0], preferred_element_type=F32) * route[:, 0:1]

    lower = iota((8, LANES), 0) < 4
    pairs = []
    for b in range(0, blocks, 2):
        left = result[:, b * LANES : (b + 1) * LANES]
        right = result[:, (b + 1) * LANES : (b + 2) * LANES]
        pairs.append(jnp.where(lower, left, pltpu.roll(right, 4, 0)))
    mixed = swap(jnp.concatenate(pairs, axis=0))
    head = lax.axis_index("head")
    group = iota(mixed.shape, 1) // 16 % heads
    moved = pltpu.roll(summed, jnp.where(head % 2 == 0, 16, LANES - 16), 1)
    for target in range(heads):
        carried = jnp.where(target == head, moved, summed)
        out[pl.ds(target * half, half), :] = jnp.where(group == target, mixed, carried).astype(BF16)


def finish(pieces, turned, after, out):
    half = turned.shape[1]
    rows, width = out.shape
    heads = pieces.shape[0] // half
    head = lax.axis_index("head")
    group = iota((rows, LANES), 1) // 16 % heads
    none = jnp.zeros((rows, LANES), F32)
    mixture, own, beside = [none, none], [none, none], [none, none]
    for source in range(heads):
        got = jnp.dot(turned[...], pieces[source * half : (source + 1) * half], preferred_element_type=F32)
        here = (group == source) & (head != source)
        next_to = (group == source ^ 1) & (head == source)
        for i in range(2):
            carried = got[(2 + i) * rows : (3 + i) * rows]
            mixture[i] = mixture[i] + got[i * rows : (i + 1) * rows]
            own[i] = own[i] + jnp.where(here, carried, 0.0)
            beside[i] = beside[i] + jnp.where(next_to, carried, 0.0)
    mixture, own, beside = [left + pltpu.roll(right, 64, 1) for left, right in (mixture, own, beside)]
    own = own + pltpu.roll(beside, jnp.where(head % 2 == 0, LANES - 16, 16), 1)
    after[...] = own[:, : after.shape[1]].astype(BF16)
    shift = (LANES - width * head) % LANES
    out[...] = pltpu.roll(mixture + own, shift, 1)[:, :width].astype(BF16)


def exchange(x, axis):
    return lax.all_to_all(x, axis, 0, 0, tiled=True)


def local(
    queries,
    keys,
    values,
    lengths,
    residual,
    out_weight,
    norm_gain,
    expert_ids,
    expert_gates,
    gate_weight,
    up_weight,
    down_weight,
):
    far, near, head = lax.axis_size("far"), lax.axis_size("near"), lax.axis_size("head")
    seq = far * near
    rows = queries.shape[0]
    later = [out_weight.T, residual, norm_gain.reshape(1, -1)]
    weight, residual, gain, parts, pick, turned, route = call(
        attend,
        [(a.shape, a.dtype) for a in later]
        + [((near * PIECE, LANES), BF16)]
        + [((seq * 2, 2 * rows), BF16), ((4 * rows, seq * 2), BF16), ((8, LANES), F32)],
        [lengths, queries, keys, values, expert_ids.T, expert_gates.T, *later],
        hbm=range(6 + len(later)),
        scratch=[
            pltpu.SMEM(lengths.shape, lengths.dtype),
            pltpu.VMEM(queries.shape, BF16),
            pltpu.VMEM(keys.shape, BF16),
            pltpu.VMEM(values.shape, BF16),
            pltpu.VMEM(expert_ids.shape[::-1], expert_ids.dtype),
            pltpu.VMEM(expert_gates.shape[::-1], F32),
            pltpu.VMEM((queries.shape[1] // HD * rows, HD), F32),
            pltpu.SemaphoreType.DMA((6 + len(later),)),
        ],
    )
    parts = exchange(parts, "near")
    cost = pl.CostEstimate(flops=1 << 33, bytes_accessed=1 << 25, transcendentals=0)
    (parts,) = call(combine, [((far * PIECE, LANES), BF16)], [parts], cost=cost)
    parts = exchange(parts, "far")
    (joined,) = call(complete, [((near * PAIRS, LANES), BF16)], [parts], cost=cost)
    joined = exchange(joined, "near")
    (chosen,) = call(
        project,
        [((head * seq * 2, LANES), BF16)],
        [joined, weight, residual, pick],
        scratch=[pltpu.VMEM((near * PAIRS, LANES), F32)],
        cost=cost,
    )
    chosen = exchange(chosen, ("head", "far", "near"))
    (outputs,) = call(
        experts,
        [((head * seq * 2, LANES), BF16)],
        [chosen, gain, gate_weight, up_weight, down_weight, route],
    )
    outputs = exchange(outputs, ("head", "far", "near"))
    return call(
        finish,
        [(residual.shape, BF16), ((rows, residual.shape[1] // head), BF16)],
        [outputs, turned],
        results=(0, 1),
    )


def solution(mesh):
    seq, head = mesh.shape["seq"], mesh.shape["head"]
    mesh = Mesh(mesh.devices.reshape(seq // NEAR, NEAR, head), ("far", "near", "head"))
    seq = ("far", "near")
    in_specs = (
        P(None, "head"),
        P(None, seq, "head"),
        P(None, seq, "head"),
        P(),
        P(None, seq),
        P("head", seq),
        P(),
        P(),
        P(),
        P(seq, None, "head"),
        P(seq, None, "head"),
        P(seq, "head", None),
    )
    out_specs = (P(None, seq), P(None, (*seq, "head")))
    return jax.shard_map(local, mesh=mesh, in_specs=in_specs, out_specs=out_specs, check_vma=False)
```

```python
import math

import jax
import jax.numpy as jnp
from jax import lax
from jax.experimental import pallas as pl
from jax.experimental.pallas import tpu as pltpu
from jax.sharding import Mesh
from jax.sharding import PartitionSpec as P

HD = 128
LANES = 128
NEAR = 8
PAIRS = 32
PIECE = PAIRS + PAIRS // 4
MASKED = -1e30
F32 = jnp.float32
BF16 = jnp.bfloat16
NT = (((1,), (1,)), ((), ()))


def iota(shape, dim):
    return lax.broadcasted_iota(jnp.int32, shape, dim)


def call(body, outs, args, hbm=(), results=(), scratch=(), limit=16 << 20, cost=None):
    spaces = [pltpu.HBM if i in hbm else pltpu.VMEM for i in range(len(args))]
    args = [pltpu.with_memory_space_constraint(a, s) if s is pltpu.HBM else a for a, s in zip(args, spaces)]
    return pl.pallas_call(
        body,
        out_shape=[
            jax.ShapeDtypeStruct(shape, dtype) if i in results else pltpu.VMEM(shape, dtype)
            for i, (shape, dtype) in enumerate(outs)
        ],
        in_specs=[pl.BlockSpec(memory_space=s) for s in spaces],
        out_specs=[pl.BlockSpec(memory_space=pltpu.VMEM) for _ in outs],
        scratch_shapes=list(scratch),
        compiler_params=pltpu.CompilerParams(vmem_limit_bytes=limit),
        cost_estimate=cost,
    )(*args)


def attend(lengths_hbm, q_hbm, k_hbm, v_hbm, ids_hbm, gates_hbm, *refs):
    lengths, q, k, v, ids, gates, wide, sems = refs[-8:]
    later = (len(refs) - 12) // 2
    out, pick, turned, route = refs[2 * later : -8]
    rows, heads = q.shape[0], q.shape[1] // HD
    pairs = [(ids_hbm, ids), (gates_hbm, gates), (q_hbm, q), (k_hbm, k), (lengths_hbm, lengths), (v_hbm, v)]
    pairs += [(refs[i], refs[later + i]) for i in range(later)]
    fetch = [pltpu.make_async_copy(far, near, sems.at[i]) for i, (far, near) in enumerate(pairs)]
    for copy in fetch:
        copy.start()
    fetch[0].wait()
    fetch[1].wait()
    routing(ids[...], gates[...], pick, turned, route)
    for copy in fetch[2:6]:
        copy.wait()
    for h in range(heads):
        wide[pl.ds(h * rows, rows), :] = q[:, h * HD : (h + 1) * HD].astype(F32)
    scores = [
        lax.dot_general(
            wide[pl.ds(r, heads, stride=rows), :].astype(BF16), k[r], NT, preferred_element_type=F32
        )
        for r in range(rows)
    ]
    scores = jnp.concatenate(scores, axis=0) * (1.0 / math.sqrt(HD))
    place = own_block() * k.shape[1] + iota((heads, k.shape[1]), 1)
    valid = jnp.concatenate([place < lengths[r] for r in range(rows)], axis=0)
    top = jnp.max(jnp.where(valid, scores, MASKED), axis=1, keepdims=True).astype(BF16).astype(F32)
    weights = jnp.where(valid, jnp.exp(scores - top), 0.0).astype(BF16)
    total = jnp.sum(weights.astype(F32), axis=1, keepdims=True)
    numer = [
        jnp.dot(weights[r * heads : (r + 1) * heads], v[r], preferred_element_type=F32)
        for r in range(rows)
    ]
    out[...] = joint(jnp.concatenate(numer, axis=0), top, total, out.shape[0] // PIECE)
    for copy in fetch[6:]:
        copy.wait()


def routing(ids, gates, pick, turned, route):
    chosen = selection(ids, pick.shape[0] // 2)
    pick[...] = chosen.astype(BF16)
    first = jnp.concatenate([ids[0:1, :], ids[0:1, :]], axis=1) == iota(chosen.shape, 0) // 2
    first = jnp.where(first, chosen, 0.0)
    both = jnp.concatenate([chosen, first, jnp.zeros((pick.shape[0], LANES - 2 * pick.shape[1]), F32)], axis=1)
    turned[...] = both.T[: turned.shape[0]].astype(BF16)

    rows = ids.shape[1]
    mine = ids == own_block()
    gate = jnp.sum(jnp.where(mine, gates, 0.0), axis=0, keepdims=True)
    here = jnp.broadcast_to(jnp.max(mine.astype(F32), axis=0, keepdims=True), (8, rows))
    before = (iota((rows, rows), 0) < iota((rows, rows), 1)).astype(F32)
    rank = jnp.dot(here, before, preferred_element_type=F32)
    taken = (rank == iota((8, rows), 0).astype(F32)) & (here > 0.0)
    weight = jnp.sum(jnp.where(taken, gate, 0.0), axis=1, keepdims=True)
    route[...] = jnp.broadcast_to(weight, route.shape)


def own_block():
    return lax.axis_index("far") * lax.axis_size("near") + lax.axis_index("near")


def joint(numer, top, total, count):
    lane = iota(numer.shape, 1)
    high = total.astype(BF16).astype(F32)
    part = lane % 32
    stats = jnp.where(part < 16, top, jnp.where(part < 24, high, total - high))
    lane = iota((8, LANES), 1)
    pieces = []
    for i in range(count):
        quarters = [stats[i * PAIRS + 8 * a : i * PAIRS + 8 * a + 8] for a in range(PAIRS // 8)]
        packed = quarters[-1]
        for a in range(PAIRS // 8 - 1):
            packed = jnp.where(lane // 32 == a, quarters[a], packed)
        pieces += [numer[i * PAIRS : (i + 1) * PAIRS], packed]
    return jnp.concatenate(pieces, axis=0).astype(BF16)


def merged(pieces):
    wide = pieces.astype(F32)
    parts = [wide[i : i + PIECE] for i in range(0, pieces.shape[0], PIECE)]
    packed = [part[PAIRS:] for part in parts]
    top = packed[0]
    for one in packed[1:]:
        top = jnp.maximum(top, one)
    numers, totals = jnp.zeros((PAIRS, LANES), F32), jnp.zeros((8, LANES), F32)
    for part, one in zip(parts, packed):
        scale = jnp.exp(one - top)
        totals = totals + pltpu.roll(scale, 16, 1) * one
        column = jnp.concatenate(
            [jnp.broadcast_to(scale[:, a : a + 1], (8, LANES)) for a in range(0, LANES, 32)], axis=0
        )
        numers = numers + column * part[:PAIRS]
    return numers, top, totals + pltpu.roll(totals, LANES - 8, 1)


def combine(parts, out):
    numer, top, total = merged(parts[...])
    part = iota(top.shape, 1) % 32
    high = total.astype(BF16).astype(F32)
    packed = jnp.where(part < 16, top, jnp.where(part < 24, high, pltpu.roll(total - high, 8, 1)))
    out[...] = jnp.concatenate([numer, packed] * (out.shape[0] // PIECE), axis=0).astype(BF16)


def complete(parts, out):
    numer, _, total = merged(parts[...])
    column = jnp.concatenate(
        [jnp.broadcast_to(total[:, a : a + 1], (8, LANES)) for a in range(16, LANES, 32)], axis=0
    )
    out[...] = jnp.concatenate([(numer / column).astype(BF16)] * (out.shape[0] // PAIRS), axis=0)


def project(pieces, weight, residual, pick, out, wide):
    rows = residual.shape[0]
    heads = pieces.shape[0] // rows
    wide[...] = pieces[...].astype(F32)
    lhs = jnp.concatenate(
        [wide[pl.ds(h, rows, stride=heads), :].astype(BF16) for h in range(heads)], axis=1
    )
    depth = lhs.shape[1] // 4
    quarters = [
        lax.dot_general(lhs[:, i : i + depth], weight[:, i : i + depth], NT, preferred_element_type=F32)
        for i in range(0, lhs.shape[1], depth)
    ]
    part = (quarters[0] + quarters[1]) + (quarters[2] + quarters[3])
    part = part + jnp.where(lax.axis_index("head") == 0, residual[...].astype(F32), 0.0)
    none = jnp.zeros_like(part)
    twice = jnp.concatenate(
        [jnp.concatenate([part, none], axis=1), jnp.concatenate([none, part], axis=1)], axis=0
    ).astype(BF16)
    send = jnp.dot(pick[...], twice, preferred_element_type=F32).astype(BF16)
    out[...] = jnp.concatenate([send] * (out.shape[0] // send.shape[0]), axis=0)


def selection(ids, count):
    top_k, rows = ids.shape
    shape = (count * 2, 2 * rows)
    expert = iota(shape, 0) // 2
    wide = jnp.concatenate([ids, ids], axis=1)
    hit = expert == wide[0:1, :]
    for k in range(1, top_k):
        hit = hit | (expert == wide[k : k + 1, :])
    hit = hit.astype(F32)
    square = (2 * rows, 2 * rows)
    before = (iota(square, 0) < iota(square, 1) % rows).astype(F32)
    rank = jnp.dot(hit, before, preferred_element_type=F32)
    slot = iota(shape, 0) % 2 + 2 * (iota(shape, 1) // rows)
    return jnp.where(rank == slot.astype(F32), hit, 0.0)


def swap(y):
    count = y.shape[0]
    row = iota(y.shape, 0) % 4
    lane = iota(y.shape, 1)
    z = pltpu.roll(y, 64, 1)
    up = pltpu.roll(z, count - 2, 0)
    down = pltpu.roll(z, 2, 0)
    return jnp.where(lane < 64, jnp.where(row < 2, y, down), jnp.where(row < 2, up, y))


def experts(pieces, gain, gate, up, down, route, out):
    width = gain.shape[1]
    blocks = width // LANES
    half = 2 * lax.axis_size("far") * lax.axis_size("near")
    heads = pieces.shape[0] // half
    summed = pieces[:half].astype(F32)
    for i in range(1, heads):
        summed = summed + pieces[i * half : (i + 1) * half].astype(F32)
    summed = summed.astype(BF16).astype(F32)
    stacked = swap(summed)
    tiles = []
    for b in range(blocks):
        tile = stacked[8 * (b // 2) : 8 * (b // 2) + 8]
        tiles.append(tile if b % 2 == 0 else pltpu.roll(tile, 4, 0))
    x = jnp.concatenate(tiles, axis=1)
    square = jnp.sum(x * x, axis=1, keepdims=True) * (1.0 / width)
    scale = lax.rsqrt(square + 1e-6)
    scaled = (x * gain[...]).astype(BF16)
    gate_proj = jnp.dot(scaled, gate[0], preferred_element_type=F32) * scale
    up_proj = jnp.dot(scaled, up[0], preferred_element_type=F32) * scale
    hidden = (gate_proj / (1.0 + jnp.exp(-gate_proj)) * up_proj).astype(BF16)
    result = jnp.dot(hidden, down[0], preferred_element_type=F32) * route[:, 0:1]

    lower = iota((8, LANES), 0) < 4
    pairs = []
    for b in range(0, blocks, 2):
        left = result[:, b * LANES : (b + 1) * LANES]
        right = result[:, (b + 1) * LANES : (b + 2) * LANES]
        pairs.append(jnp.where(lower, left, pltpu.roll(right, 4, 0)))
    mixed = swap(jnp.concatenate(pairs, axis=0))
    head = lax.axis_index("head")
    group = iota(mixed.shape, 1) // 16 % heads
    moved = pltpu.roll(summed, jnp.where(head % 2 == 0, 16, LANES - 16), 1)
    for target in range(heads):
        carried = jnp.where(target == head, moved, summed)
        out[pl.ds(target * half, half), :] = jnp.where(group == target, mixed, carried).astype(BF16)


def finish(pieces, turned, after, out):
    half = turned.shape[1]
    rows, width = out.shape
    heads = pieces.shape[0] // half
    head = lax.axis_index("head")
    group = iota((rows, LANES), 1) // 16 % heads
    none = jnp.zeros((rows, LANES), F32)
    mixture, own, beside = [none, none], [none, none], [none, none]
    for source in range(heads):
        got = jnp.dot(turned[...], pieces[source * half : (source + 1) * half], preferred_element_type=F32)
        here = (group == source) & (head != source)
        next_to = (group == source ^ 1) & (head == source)
        for i in range(2):
            carried = got[(2 + i) * rows : (3 + i) * rows]
            mixture[i] = mixture[i] + got[i * rows : (i + 1) * rows]
            own[i] = own[i] + jnp.where(here, carried, 0.0)
            beside[i] = beside[i] + jnp.where(next_to, carried, 0.0)
    mixture, own, beside = [left + pltpu.roll(right, 64, 1) for left, right in (mixture, own, beside)]
    own = own + pltpu.roll(beside, jnp.where(head % 2 == 0, LANES - 16, 16), 1)
    after[...] = own[:, : after.shape[1]].astype(BF16)
    shift = (LANES - width * head) % LANES
    out[...] = pltpu.roll(mixture + own, shift, 1)[:, :width].astype(BF16)


def exchange(x, axis):
    return lax.all_to_all(x, axis, 0, 0, tiled=True)


def local(
    queries,
    keys,
    values,
    lengths,
    residual,
    out_weight,
    norm_gain,
    expert_ids,
    expert_gates,
    gate_weight,
    up_weight,
    down_weight,
):
    far, near, head = lax.axis_size("far"), lax.axis_size("near"), lax.axis_size("head")
    seq = far * near
    rows = queries.shape[0]
    later = [out_weight.T, residual, norm_gain.reshape(1, -1)]
    weight, residual, gain, parts, pick, turned, route = call(
        attend,
        [(a.shape, a.dtype) for a in later]
        + [((near * PIECE, LANES), BF16)]
        + [((seq * 2, 2 * rows), BF16), ((4 * rows, seq * 2), BF16), ((8, LANES), F32)],
        [lengths, queries, keys, values, expert_ids.T, expert_gates.T, *later],
        hbm=range(6 + len(later)),
        scratch=[
            pltpu.SMEM(lengths.shape, lengths.dtype),
            pltpu.VMEM(queries.shape, BF16),
            pltpu.VMEM(keys.shape, BF16),
            pltpu.VMEM(values.shape, BF16),
            pltpu.VMEM(expert_ids.shape[::-1], expert_ids.dtype),
            pltpu.VMEM(expert_gates.shape[::-1], F32),
            pltpu.VMEM((queries.shape[1] // HD * rows, HD), F32),
            pltpu.SemaphoreType.DMA((6 + len(later),)),
        ],
    )
    parts = exchange(parts, "near")
    cost = pl.CostEstimate(flops=1 << 33, bytes_accessed=1 << 25, transcendentals=0)
    (parts,) = call(combine, [((far * PIECE, LANES), BF16)], [parts], cost=cost)
    parts = exchange(parts, "far")
    (joined,) = call(complete, [((near * PAIRS, LANES), BF16)], [parts], cost=cost)
    joined = exchange(joined, "near")
    (chosen,) = call(
        project,
        [((head * seq * 2, LANES), BF16)],
        [joined, weight, residual, pick],
        scratch=[pltpu.VMEM((near * PAIRS, LANES), F32)],
        cost=cost,
    )
    chosen = exchange(chosen, ("head", "far", "near"))
    (outputs,) = call(
        experts,
        [((head * seq * 2, LANES), BF16)],
        [chosen, gain, gate_weight, up_weight, down_weight, route],
    )
    outputs = exchange(outputs, ("head", "far", "near"))
    return call(
        finish,
        [(residual.shape, BF16), ((rows, residual.shape[1] // head), BF16)],
        [outputs, turned],
        results=(0, 1),
    )


def solution(mesh):
    seq, head = mesh.shape["seq"], mesh.shape["head"]
    mesh = Mesh(mesh.devices.reshape(seq // NEAR, NEAR, head), ("far", "near", "head"))
    seq = ("far", "near")
    in_specs = (
        P(None, "head"),
        P(None, seq, "head"),
        P(None, seq, "head"),
        P(),
        P(None, seq),
        P("head", seq),
        P(),
        P(),
        P(),
        P(seq, None, "head"),
        P(seq, None, "head"),
        P(seq, "head", None),
    )
    out_specs = (P(None, seq), P(None, (*seq, "head")))
    return jax.shard_map(local, mesh=mesh, in_specs=in_specs, out_specs=out_specs, check_vma=False)
```

```python
import math

import jax
import jax.numpy as jnp
from jax import lax
from jax.experimental import pallas as pl
from jax.experimental.pallas import tpu as pltpu
from jax.sharding import Mesh
from jax.sharding import PartitionSpec as P

HD = 128
LANES = 128
NEAR = 8
PAIRS = 32
PIECE = PAIRS + PAIRS // 4
MASKED = -1e30
F32 = jnp.float32
BF16 = jnp.bfloat16
NT = (((1,), (1,)), ((), ()))


def iota(shape, dim):
    return lax.broadcasted_iota(jnp.int32, shape, dim)


def call(body, outs, args, hbm=(), results=(), scratch=(), limit=16 << 20, cost=None):
    spaces = [pltpu.HBM if i in hbm else pltpu.VMEM for i in range(len(args))]
    args = [pltpu.with_memory_space_constraint(a, s) if s is pltpu.HBM else a for a, s in zip(args, spaces)]
    return pl.pallas_call(
        body,
        out_shape=[
            jax.ShapeDtypeStruct(shape, dtype) if i in results else pltpu.VMEM(shape, dtype)
            for i, (shape, dtype) in enumerate(outs)
        ],
        in_specs=[pl.BlockSpec(memory_space=s) for s in spaces],
        out_specs=[pl.BlockSpec(memory_space=pltpu.VMEM) for _ in outs],
        scratch_shapes=list(scratch),
        compiler_params=pltpu.CompilerParams(vmem_limit_bytes=limit),
        cost_estimate=cost,
    )(*args)


def attend(lengths_hbm, q_hbm, k_hbm, v_hbm, ids_hbm, gates_hbm, *refs):
    lengths, q, k, v, ids, gates, wide, sems = refs[-8:]
    later = (len(refs) - 12) // 2
    out, pick, turned, route = refs[2 * later : -8]
    rows, heads = q.shape[0], q.shape[1] // HD
    pairs = [(ids_hbm, ids), (gates_hbm, gates), (q_hbm, q), (k_hbm, k), (lengths_hbm, lengths), (v_hbm, v)]
    pairs += [(refs[i], refs[later + i]) for i in range(later)]
    fetch = [pltpu.make_async_copy(far, near, sems.at[i]) for i, (far, near) in enumerate(pairs)]
    for copy in fetch:
        copy.start()
    fetch[0].wait()
    fetch[1].wait()
    routing(ids[...], gates[...], pick, turned, route)
    for copy in fetch[2:6]:
        copy.wait()
    for h in range(heads):
        wide[pl.ds(h * rows, rows), :] = q[:, h * HD : (h + 1) * HD].astype(F32)
    scores = [
        lax.dot_general(
            wide[pl.ds(r, heads, stride=rows), :].astype(BF16), k[r], NT, preferred_element_type=F32
        )
        for r in range(rows)
    ]
    scores = jnp.concatenate(scores, axis=0) * (1.0 / math.sqrt(HD))
    place = own_block() * k.shape[1] + iota((heads, k.shape[1]), 1)
    valid = jnp.concatenate([place < lengths[r] for r in range(rows)], axis=0)
    top = jnp.max(jnp.where(valid, scores, MASKED), axis=1, keepdims=True).astype(BF16).astype(F32)
    weights = jnp.where(valid, jnp.exp(scores - top), 0.0).astype(BF16)
    total = jnp.sum(weights.astype(F32), axis=1, keepdims=True)
    numer = [
        jnp.dot(weights[r * heads : (r + 1) * heads], v[r], preferred_element_type=F32)
        for r in range(rows)
    ]
    out[...] = joint(jnp.concatenate(numer, axis=0), top, total, out.shape[0] // PIECE)
    for copy in fetch[6:]:
        copy.wait()


def routing(ids, gates, pick, turned, route):
    chosen = selection(ids, pick.shape[0] // 2)
    pick[...] = chosen.astype(BF16)
    first = jnp.concatenate([ids[0:1, :], ids[0:1, :]], axis=1) == iota(chosen.shape, 0) // 2
    first = jnp.where(first, chosen, 0.0)
    both = jnp.concatenate([chosen, first, jnp.zeros((pick.shape[0], LANES - 2 * pick.shape[1]), F32)], axis=1)
    turned[...] = both.T[: turned.shape[0]].astype(BF16)

    rows = ids.shape[1]
    mine = ids == own_block()
    gate = jnp.sum(jnp.where(mine, gates, 0.0), axis=0, keepdims=True)
    here = jnp.broadcast_to(jnp.max(mine.astype(F32), axis=0, keepdims=True), (8, rows))
    before = (iota((rows, rows), 0) < iota((rows, rows), 1)).astype(F32)
    rank = jnp.dot(here, before, preferred_element_type=F32)
    taken = (rank == iota((8, rows), 0).astype(F32)) & (here > 0.0)
    weight = jnp.sum(jnp.where(taken, gate, 0.0), axis=1, keepdims=True)
    route[...] = jnp.broadcast_to(weight, route.shape)


def own_block():
    return lax.axis_index("far") * lax.axis_size("near") + lax.axis_index("near")


def joint(numer, top, total, count):
    lane = iota(numer.shape, 1)
    high = total.astype(BF16).astype(F32)
    part = lane % 32
    stats = jnp.where(part < 16, top, jnp.where(part < 24, high, total - high))
    lane = iota((8, LANES), 1)
    pieces = []
    for i in range(count):
        quarters = [stats[i * PAIRS + 8 * a : i * PAIRS + 8 * a + 8] for a in range(PAIRS // 8)]
        packed = quarters[-1]
        for a in range(PAIRS // 8 - 1):
            packed = jnp.where(lane // 32 == a, quarters[a], packed)
        pieces += [numer[i * PAIRS : (i + 1) * PAIRS], packed]
    return jnp.concatenate(pieces, axis=0).astype(BF16)


def merged(pieces):
    wide = pieces.astype(F32)
    parts = [wide[i : i + PIECE] for i in range(0, pieces.shape[0], PIECE)]
    packed = [part[PAIRS:] for part in parts]
    top = packed[0]
    for one in packed[1:]:
        top = jnp.maximum(top, one)
    numers, totals = jnp.zeros((PAIRS, LANES), F32), jnp.zeros((8, LANES), F32)
    for part, one in zip(parts, packed):
        scale = jnp.exp(one - top)
        totals = totals + pltpu.roll(scale, 16, 1) * one
        column = jnp.concatenate(
            [jnp.broadcast_to(scale[:, a : a + 1], (8, LANES)) for a in range(0, LANES, 32)], axis=0
        )
        numers = numers + column * part[:PAIRS]
    return numers, top, totals + pltpu.roll(totals, LANES - 8, 1)


def combine(parts, out):
    numer, top, total = merged(parts[...])
    part = iota(top.shape, 1) % 32
    high = total.astype(BF16).astype(F32)
    packed = jnp.where(part < 16, top, jnp.where(part < 24, high, pltpu.roll(total - high, 8, 1)))
    out[...] = jnp.concatenate([numer, packed] * (out.shape[0] // PIECE), axis=0).astype(BF16)


def complete(parts, out):
    numer, _, total = merged(parts[...])
    column = jnp.concatenate(
        [jnp.broadcast_to(total[:, a : a + 1], (8, LANES)) for a in range(16, LANES, 32)], axis=0
    )
    out[...] = jnp.concatenate([(numer / column).astype(BF16)] * (out.shape[0] // PAIRS), axis=0)


def project(pieces, weight, residual, pick, out, wide):
    rows = residual.shape[0]
    heads = pieces.shape[0] // rows
    wide[...] = pieces[...].astype(F32)
    lhs = jnp.concatenate(
        [wide[pl.ds(h, rows, stride=heads), :].astype(BF16) for h in range(heads)], axis=1
    )
    depth = lhs.shape[1] // 8
    sums = [
        lax.dot_general(lhs[:, i : i + depth], weight[:, i : i + depth], NT, preferred_element_type=F32)
        for i in range(0, lhs.shape[1], depth)
    ]
    while len(sums) > 1:
        sums = [left + right for left, right in zip(sums[::2], sums[1::2])]
    part = sums[0]
    part = part + jnp.where(lax.axis_index("head") == 0, residual[...].astype(F32), 0.0)
    none = jnp.zeros_like(part)
    twice = jnp.concatenate(
        [jnp.concatenate([part, none], axis=1), jnp.concatenate([none, part], axis=1)], axis=0
    ).astype(BF16)
    send = jnp.dot(pick[...], twice, preferred_element_type=F32).astype(BF16)
    out[...] = jnp.concatenate([send] * (out.shape[0] // send.shape[0]), axis=0)


def selection(ids, count):
    top_k, rows = ids.shape
    shape = (count * 2, 2 * rows)
    expert = iota(shape, 0) // 2
    wide = jnp.concatenate([ids, ids], axis=1)
    hit = expert == wide[0:1, :]
    for k in range(1, top_k):
        hit = hit | (expert == wide[k : k + 1, :])
    hit = hit.astype(F32)
    square = (2 * rows, 2 * rows)
    before = (iota(square, 0) < iota(square, 1) % rows).astype(F32)
    rank = jnp.dot(hit, before, preferred_element_type=F32)
    slot = iota(shape, 0) % 2 + 2 * (iota(shape, 1) // rows)
    return jnp.where(rank == slot.astype(F32), hit, 0.0)


def swap(y):
    count = y.shape[0]
    row = iota(y.shape, 0) % 4
    lane = iota(y.shape, 1)
    z = pltpu.roll(y, 64, 1)
    up = pltpu.roll(z, count - 2, 0)
    down = pltpu.roll(z, 2, 0)
    return jnp.where(lane < 64, jnp.where(row < 2, y, down), jnp.where(row < 2, up, y))


def experts(pieces, gain, gate, up, down, route, out):
    width = gain.shape[1]
    blocks = width // LANES
    half = 2 * lax.axis_size("far") * lax.axis_size("near")
    heads = pieces.shape[0] // half
    summed = pieces[:half].astype(F32)
    for i in range(1, heads):
        summed = summed + pieces[i * half : (i + 1) * half].astype(F32)
    summed = summed.astype(BF16).astype(F32)
    stacked = swap(summed)
    tiles = []
    for b in range(blocks):
        tile = stacked[8 * (b // 2) : 8 * (b // 2) + 8]
        tiles.append(tile if b % 2 == 0 else pltpu.roll(tile, 4, 0))
    x = jnp.concatenate(tiles, axis=1)
    square = jnp.sum(x * x, axis=1, keepdims=True) * (1.0 / width)
    scale = lax.rsqrt(square + 1e-6)
    scaled = (x * gain[...]).astype(BF16)
    gate_proj = jnp.dot(scaled, gate[0], preferred_element_type=F32) * scale
    up_proj = jnp.dot(scaled, up[0], preferred_element_type=F32) * scale
    hidden = (gate_proj / (1.0 + jnp.exp(-gate_proj)) * up_proj).astype(BF16)
    result = jnp.dot(hidden, down[0], preferred_element_type=F32) * route[:, 0:1]

    lower = iota((8, LANES), 0) < 4
    pairs = []
    for b in range(0, blocks, 2):
        left = result[:, b * LANES : (b + 1) * LANES]
        right = result[:, (b + 1) * LANES : (b + 2) * LANES]
        pairs.append(jnp.where(lower, left, pltpu.roll(right, 4, 0)))
    mixed = swap(jnp.concatenate(pairs, axis=0))
    head = lax.axis_index("head")
    group = iota(mixed.shape, 1) // 16 % heads
    moved = pltpu.roll(summed, jnp.where(head % 2 == 0, 16, LANES - 16), 1)
    for target in range(heads):
        carried = jnp.where(target == head, moved, summed)
        out[pl.ds(target * half, half), :] = jnp.where(group == target, mixed, carried).astype(BF16)


def finish(pieces, turned, after, out):
    half = turned.shape[1]
    rows, width = out.shape
    heads = pieces.shape[0] // half
    head = lax.axis_index("head")
    group = iota((rows, LANES), 1) // 16 % heads
    none = jnp.zeros((rows, LANES), F32)
    mixture, own, beside = [none, none], [none, none], [none, none]
    for source in range(heads):
        got = jnp.dot(turned[...], pieces[source * half : (source + 1) * half], preferred_element_type=F32)
        here = (group == source) & (head != source)
        next_to = (group == source ^ 1) & (head == source)
        for i in range(2):
            carried = got[(2 + i) * rows : (3 + i) * rows]
            mixture[i] = mixture[i] + got[i * rows : (i + 1) * rows]
            own[i] = own[i] + jnp.where(here, carried, 0.0)
            beside[i] = beside[i] + jnp.where(next_to, carried, 0.0)
    mixture, own, beside = [left + pltpu.roll(right, 64, 1) for left, right in (mixture, own, beside)]
    own = own + pltpu.roll(beside, jnp.where(head % 2 == 0, LANES - 16, 16), 1)
    after[...] = own[:, : after.shape[1]].astype(BF16)
    shift = (LANES - width * head) % LANES
    out[...] = pltpu.roll(mixture + own, shift, 1)[:, :width].astype(BF16)


def exchange(x, axis):
    return lax.all_to_all(x, axis, 0, 0, tiled=True)


def local(
    queries,
    keys,
    values,
    lengths,
    residual,
    out_weight,
    norm_gain,
    expert_ids,
    expert_gates,
    gate_weight,
    up_weight,
    down_weight,
):
    far, near, head = lax.axis_size("far"), lax.axis_size("near"), lax.axis_size("head")
    seq = far * near
    rows = queries.shape[0]
    later = [out_weight.T, residual, norm_gain.reshape(1, -1)]
    weight, residual, gain, parts, pick, turned, route = call(
        attend,
        [(a.shape, a.dtype) for a in later]
        + [((near * PIECE, LANES), BF16)]
        + [((seq * 2, 2 * rows), BF16), ((4 * rows, seq * 2), BF16), ((8, LANES), F32)],
        [lengths, queries, keys, values, expert_ids.T, expert_gates.T, *later],
        hbm=range(6 + len(later)),
        scratch=[
            pltpu.SMEM(lengths.shape, lengths.dtype),
            pltpu.VMEM(queries.shape, BF16),
            pltpu.VMEM(keys.shape, BF16),
            pltpu.VMEM(values.shape, BF16),
            pltpu.VMEM(expert_ids.shape[::-1], expert_ids.dtype),
            pltpu.VMEM(expert_gates.shape[::-1], F32),
            pltpu.VMEM((queries.shape[1] // HD * rows, HD), F32),
            pltpu.SemaphoreType.DMA((6 + len(later),)),
        ],
    )
    parts = exchange(parts, "near")
    cost = pl.CostEstimate(flops=1 << 33, bytes_accessed=1 << 25, transcendentals=0)
    (parts,) = call(combine, [((far * PIECE, LANES), BF16)], [parts], cost=cost)
    parts = exchange(parts, "far")
    (joined,) = call(complete, [((near * PAIRS, LANES), BF16)], [parts], cost=cost)
    joined = exchange(joined, "near")
    (chosen,) = call(
        project,
        [((head * seq * 2, LANES), BF16)],
        [joined, weight, residual, pick],
        scratch=[pltpu.VMEM((near * PAIRS, LANES), F32)],
        cost=cost,
    )
    chosen = exchange(chosen, ("head", "far", "near"))
    (outputs,) = call(
        experts,
        [((head * seq * 2, LANES), BF16)],
        [chosen, gain, gate_weight, up_weight, down_weight, route],
    )
    outputs = exchange(outputs, ("head", "far", "near"))
    return call(
        finish,
        [(residual.shape, BF16), ((rows, residual.shape[1] // head), BF16)],
        [outputs, turned],
        results=(0, 1),
    )


def solution(mesh):
    seq, head = mesh.shape["seq"], mesh.shape["head"]
    mesh = Mesh(mesh.devices.reshape(seq // NEAR, NEAR, head), ("far", "near", "head"))
    seq = ("far", "near")
    in_specs = (
        P(None, "head"),
        P(None, seq, "head"),
        P(None, seq, "head"),
        P(),
        P(None, seq),
        P("head", seq),
        P(),
        P(),
        P(),
        P(seq, None, "head"),
        P(seq, None, "head"),
        P(seq, "head", None),
    )
    out_specs = (P(None, seq), P(None, (*seq, "head")))
    return jax.shard_map(local, mesh=mesh, in_specs=in_specs, out_specs=out_specs, check_vma=False)
```
